512 devices in a mesh: amp: 8 (over y), int: 16 (over z, core), rep: 4 (over x).
Axes of the slice: x: 4, y: 8, z: 8, core: 2. Of those that a mesh axis runs over, the one named last changes fastest.
Arguments:
- amplitudes: bfloat16 [32, 1024, 4096], P('int', 'amp', 'rep'), may hold values from -6 to 6
- pp_blocks: bfloat16 [4, 128, 128, 128], P('rep', 'int'), may hold values from -0.5 to 0.5
- src_tiles: int32 [4, 128], P('rep', 'int'), may hold values from 0 to 7
- src_wins: int32 [4, 128], P('rep', 'int'), may hold values from 0 to 31
- dst_tiles: int32 [4, 128], P('rep', 'int'), may hold values from 0 to 31
- dst_wins: int32 [4, 128], P('rep', 'int'), may hold values from 0 to 1
- hh_integrals: bfloat16 [1024, 1024], replicated, may hold values from -0.1875 to 0.1875
- pair_gap: float32 [1024], P('amp'), may hold values from 0.5 to 2
- vir_energy: float32 [4096], P('rep'), may hold values from 0.5 to 2
- win_energy: float32 [32], P('int'), may hold values from 0.5 to 2
Outputs:
- amp_update: float32 [32, 1024, 4096], P('int', 'amp', 'rep')
The draws below stay inside these ranges and needn't reach their ends.
Inputs may be any that keep to these rules, and one draw needn't show every extreme that they name: `dst_wins`: output second virtual index within the block's group; block k belongs to group k // 8.
All inputs are finite; a program needn't handle non-finite values.
Results may differ from the reference program's by a relative error of at most 0.0003.
Values may be sent and summed in bfloat16 or wider, within the bound.
A program may use at most 64 MiB of HBM per device.

```python
import math
import jax
import jax.numpy as jnp
from jax import lax

TILE = 128
NT = 32
BW_DEV = 2
NB_DEV = 8
NV = 4096
NT_REP = 8
PAIRS = 1024
BW = 32
NBG = 128
N_REP = 4


def place_ends(result, own_key, smallest, high):
    longest = result.shape.index(max(result.shape))
    spots = []
    for shift in (0, 1):
        where = [jax.random.randint(jax.random.fold_in(own_key, axis), (), 0, length) for axis, length in enumerate(result.shape)]
        where[longest] = (where[longest] + shift) % result.shape[longest]
        spots.append(tuple(where))
    return result.at[spots[0]].set(smallest).at[spots[1]].set(high)


def block_levels(stream_key, shape, split, low, high):
    def one(dim, parts):
        steps = jax.random.uniform(jax.random.fold_in(jax.random.fold_in(stream_key, 6), dim), (parts,), jnp.float32, low / len(split), high / len(split))
        return jnp.repeat(jnp.exp(steps), shape[dim] // parts).reshape((-1,) + (1,) * (len(shape) - dim - 1))

    loudness = one(*split[0])
    for cut in split[1:]:
        loudness = loudness * one(*cut)
    return loudness


def noise(own_key, extent, spread, limit, shards=(), held_as=jnp.bfloat16):
    drawn = jax.random.normal(own_key, extent, jnp.float32) * spread
    if len(shards) > 0:
        drawn = block_levels(own_key, extent, shards, -0.22, 0.18) * drawn
    return jnp.clip(drawn, min=-limit, max=limit).astype(held_as)


def setup_inputs(seed: int = 0) -> dict:
    streams_of = jax.random.split(jax.random.key(seed), 11)
    return {
        "amplitudes": noise(streams_of[0], (BW, PAIRS, NV), 1.0, 6.0, ((0, 16), (1, 8), (2, 4))),
        "pp_blocks": noise(streams_of[1], (N_REP, NBG, TILE, TILE), TILE ** -0.5, 0.5, ((0, 4), (1, 16))),
        "src_tiles": place_ends(jax.random.randint(streams_of[2], (N_REP, NBG), 0, NT_REP), jax.random.fold_in(streams_of[2], 1), 0, NT_REP - 1).astype(jnp.int32),
        "src_wins": place_ends(jax.random.randint(streams_of[3], (N_REP, NBG), 0, BW), jax.random.fold_in(streams_of[3], 1), 0, BW - 1).astype(jnp.int32),
        "dst_tiles": place_ends(jax.random.randint(streams_of[4], (N_REP, NBG), 0, NT), jax.random.fold_in(streams_of[4], 1), 0, NT - 1).astype(jnp.int32),
        "dst_wins": place_ends(jax.random.randint(streams_of[5], (N_REP, NBG), 0, BW_DEV), jax.random.fold_in(streams_of[5], 1), 0, BW_DEV - 1).astype(jnp.int32),
        "hh_integrals": noise(streams_of[6], (PAIRS, PAIRS), PAIRS ** -0.5, 0.1875),
        "pair_gap": jnp.clip(jnp.exp(math.log(2.0) - 1.3862944 * jax.random.uniform(streams_of[7], (PAIRS,), jnp.float32) ** block_levels(streams_of[7], (PAIRS,), ((0, 8),), -0.2, 0.2)), 0.5, 2.0),
        "vir_energy": jnp.clip(jnp.exp(math.log(2.0) - 1.3862944 * jax.random.uniform(streams_of[8], (NV,), jnp.float32) ** block_levels(streams_of[8], (NV,), ((0, 4),), -0.2, 0.2)), 0.5, 2.0),
        "win_energy": jnp.clip(jnp.exp(math.log(2.0) - 1.3862944 * jax.random.uniform(streams_of[9], (BW,), jnp.float32) ** block_levels(streams_of[9], (BW,), ((0, 16),), -0.2, 0.2)), 0.5, 2.0),
    }


def reference(amplitudes, pp_blocks, src_tiles, src_wins, dst_tiles, dst_wins, hh_integrals, pair_gap, vir_energy, win_energy):
    count = N_REP * NBG
    blocks = pp_blocks.reshape(count, TILE, TILE)
    offsets = (jnp.arange(N_REP, dtype=jnp.int32) * NT_REP)[:, None]
    col_tile = (src_tiles + offsets).reshape(count).astype(jnp.int32)
    win_base = ((jnp.arange(NBG, dtype=jnp.int32) // NB_DEV) * BW_DEV)[None, :]
    out_win = (dst_wins + win_base).reshape(count).astype(jnp.int32)
    in_win = src_wins.reshape(count).astype(jnp.int32)
    out_tile = dst_tiles.reshape(count).astype(jnp.int32)
    zero = jnp.zeros((), jnp.int32)

    def add_block(index, total):
        columns = lax.dynamic_slice(amplitudes, (in_win[index], zero, col_tile[index] * TILE), (1, PAIRS, TILE))[0]
        product = jnp.dot(columns, blocks[index], preferred_element_type=jnp.float32)
        place = (out_win[index], zero, out_tile[index] * TILE)
        current = lax.dynamic_slice(total, place, (1, PAIRS, TILE))
        return lax.dynamic_update_slice(total, current + product[None], place)

    particle = lax.fori_loop(0, count, add_block, jnp.zeros((BW, PAIRS, NV), jnp.float32))
    hole = lax.map(lambda slab: jnp.dot(hh_integrals, slab, preferred_element_type=jnp.float32), amplitudes)
    denom = win_energy[:, None, None] + pair_gap[None, :, None] + vir_energy[None, None, :]
    return (particle + hole) / denom
```

```python
import functools

import jax
import jax.numpy as jnp
from jax import lax
from jax.experimental import pallas as pl
from jax.experimental.pallas import tpu as pltpu
from jax.sharding import PartitionSpec as P

MESH = pl.DeviceIdType.MESH
CHUNK = 1
GAP = 5
LEVELS = 32760.0
LEAST = 1e-33


def hops(direction, chain, nz):
    return nz // 2 - ((chain + direction) % 2)


def z_order(nz, chains):
    order = []
    lists = []
    for direction in (0, 1):
        sent = {j: 0 for j in range(chains)}
        last = {j: -GAP for j in range(chains)}
        seq = []
        tick = 0
        while any(sent[j] < hops(direction, j, nz) for j in sent):
            ready = [j for j in sent if sent[j] < hops(direction, j, nz) and tick - last[j] >= GAP]
            if ready:
                j = ready[0]
                seq.append((tick, direction, j, sent[j]))
                sent[j] += 1
                last[j] = tick
            tick += 1
        lists.extend(seq)
    order = sorted(lists)
    return order


def kernel(
    ny, nz, nx, chains,
    st_ref, sw_ref, dt_ref, dw_ref, amp_ref, blk_ref, h_ref, gap_ref, vir_ref, win_ref,
    out_ref,
    tab, gap, vir, win, inv, achip, x_in, hv, ball, sall, zinj, zbuf, idxv, idxs, ysend, ssend, yrecv, srecv, yown, acc, prod,
    tab_sem, amp_sem, loc_sem, sib_sem, idx_ss, idx_rs, y1_ss, y1_rs, y2_ss, y2_rs, z_ss, z_rs, b_ss, b_rs, s_ss, s_rs,
):
    width, rows, ncol = amp_ref.shape
    tile = blk_ref.shape[-1]
    tiles = ncol // tile
    per_chip = 2 * width
    slots = blk_ref.shape[1]
    y = lax.axis_index("amp")
    i = lax.axis_index("int")
    x = lax.axis_index("rep")
    z = i // 2
    core = lax.rem(i, 2)

    def ypeer(d):
        return {"amp": lax.rem(y + (d + ny) % ny, ny)}

    def zpeer(d):
        return {"int": lax.rem(i + 2 * ((d + nz) % nz), 2 * nz)}

    def xpeer(d):
        return {"rep": lax.rem(x + (d + nx) % nx, nx)}

    sibling = {"int": i + 1 - 2 * core}
    peers = [ypeer(d) for d in range(1, ny)] + [zpeer(d) for d in range(1, nz)]
    peers += [xpeer(d) for d in range(1, nx)] + [sibling]

    def remote(src, dst, ss, rs, peer):
        return pltpu.make_async_remote_copy(
            src_ref=src, dst_ref=dst, send_sem=ss, recv_sem=rs, device_id=peer, device_id_type=MESH
        )

    def span(index, size):
        return pl.ds(pl.multiple_of(index * size, size), size)

    sends = []

    def send(copy):
        copy.start()
        sends.append(copy)

    barrier = pltpu.get_barrier_semaphore()
    for peer in peers:
        pl.semaphore_signal(barrier, inc=1, device_id=peer, device_id_type=MESH)

    own_tab = [
        pltpu.make_async_copy(ref, tab.at[n], tab_sem.at[n])
        for n, ref in enumerate((st_ref, sw_ref, dt_ref, dw_ref))
    ]
    own_en = [
        pltpu.make_async_copy(ref, to, tab_sem.at[4 + n])
        for n, (ref, to) in enumerate(((gap_ref, gap), (vir_ref, vir), (win_ref, win)))
    ]
    own_amp = [
        pltpu.make_async_copy(
            amp_ref.at[:, :, t * tile : (t + 1) * tile], achip.at[t, pl.ds(core * width, width)], amp_sem.at[t]
        )
        for t in range(tiles)
    ]
    own_h = pltpu.make_async_copy(h_ref, hv, loc_sem.at[1])
    own_blk = pltpu.make_async_copy(blk_ref.at[0], ball.at[x], loc_sem.at[2])
    own_x = [
        pltpu.make_async_copy(
            amp_ref.at[b, :, span(y, tile)], x_in.at[b, span(y, rows), :], loc_sem.at[3 + b]
        )
        for b in range(width)
    ]
    for copy in own_tab + own_x + own_amp + [own_h, own_blk] + own_en:
        copy.start()
    for copy in own_tab:
        copy.wait()
    for place in (z, nz + x):
        idxv[place] = jnp.zeros(idxv.shape[1:], jnp.int32)
        for row in range(4):
            idxv[place, row : row + 1, 0:slots] = tab[row]
    pl.semaphore_wait(barrier, len(peers))

    idx_z = [remote(idxv.at[z], idxv.at[z], idx_ss.at[d], idx_rs.at[d], zpeer(d)) for d in range(1, nz)]
    idx_x = [
        remote(idxv.at[nz + x], idxv.at[nz + x], idx_ss.at[nz + d], idx_rs.at[nz + d], xpeer(d))
        for d in range(1, nx)
    ]
    for copy in idx_z:
        send(copy)
    twin = []
    for t in range(tiles):
        part = achip.at[t, pl.ds(core * width, width)]
        twin.append(
            remote(amp_ref.at[:, :, t * tile : (t + 1) * tile], part, sib_sem.at[0, t], sib_sem.at[1, t], sibling)
        )
        send(twin[t])
    far_first = sorted(range(1, ny), key=lambda d: -min(d, ny - d))
    first = {}
    for b in range(width):
        for d in far_first:
            to = lax.rem(y + d, ny)
            first[b, d] = remote(
                amp_ref.at[b, :, span(to, tile)],
                x_in.at[b, span(y, rows), :],
                y1_ss.at[b, d],
                y1_rs.at[b, d],
                ypeer(d),
            )
            send(first[b, d])
    for copy in idx_x:
        send(copy)
    shared = [remote(blk_ref.at[0], ball.at[x], b_ss.at[d], b_rs.at[d], xpeer(d)) for d in range(1, nx)]
    for copy in shared:
        send(copy)

    for copy in idx_z:
        copy.wait_recv()
    table = pltpu.make_async_copy(idxv.at[0:nz], idxs.at[0:nz], loc_sem.at[6])
    table.start()
    table.wait()
    for t in range(tiles):
        own_amp[t].wait()
        twin[t].wait_recv()

    def slab(place, slot):
        win = idxs[place, 1, slot]
        col = idxs[place, 0, slot]
        return lax.div(win, per_chip), achip[col, lax.rem(win, per_chip)]

    moves = {}

    def z_message(direction, chain, hop):
        far = hops(direction, chain, nz)
        sign = 1 - 2 * direction
        dest = lax.rem(z + (sign * (far - hop) + nz) % nz, nz)
        if hop == 0:
            buf = zinj.at[direction, chain]
        else:
            buf = zbuf.at[direction, chain, hop - 1]
            moves[direction, chain, hop - 1].wait_recv()
        for k in range(CHUNK):
            owner, value = slab(dest, chain * CHUNK + k)
            if hop > 0:
                value = jnp.where(owner == z, value, buf[k])
            buf[k] = value
        moves[direction, chain, hop] = remote(
            buf,
            zbuf.at[direction, chain, hop],
            z_ss.at[direction, chain, hop],
            z_rs.at[direction, chain, hop],
            zpeer(sign),
        )
        send(moves[direction, chain, hop])

    spread = {}

    def z_final(chain):
        last = [hops(direction, chain, nz) for direction in (0, 1)]
        for direction in (0, 1):
            moves[direction, chain, last[direction] - 1].wait_recv()
        for k in range(CHUNK):
            slot = chain * CHUNK + k
            owner, value = slab(z, slot)
            behind = lax.rem(z - owner + nz, nz)
            up = zbuf[0, chain, last[0] - 1, k]
            down = zbuf[1, chain, last[1] - 1, k]
            value = jnp.where(owner == z, value, jnp.where(behind <= last[0], up, down))
            sall[x, slot] = value
        part = sall.at[x, pl.ds(chain * CHUNK, CHUNK)]
        for d in (list(range(2, nx)) + [1]):
            spread[chain, d] = remote(part, part, s_ss.at[chain, d], s_rs.at[chain, d], xpeer(d))
            send(spread[chain, d])

    state = {"blocks": False, "own": set(), "h": False}

    def products(chain):
        if not state["blocks"]:
            own_blk.wait()
            for copy in idx_x + shared:
                copy.wait_recv()
            more = pltpu.make_async_copy(idxv.at[nz : nz + nx], idxs.at[nz : nz + nx], loc_sem.at[5])
            more.start()
            more.wait()
            state["blocks"] = True
        keys = []
        for d in range(nx):
            origin = lax.rem(x - d + nx, nx)
            if d > 0:
                spread[chain, d].wait_recv()
            for k in range(CHUNK):
                slot = chain * CHUNK + k
                prod[d * CHUNK + k] = jnp.dot(
                    sall[origin, slot], ball[origin, slot], preferred_element_type=jnp.float32
                )
                keys.append(idxs[nz + origin, 3, slot] * (tiles * nx) + idxs[nz + origin, 2, slot] - x * tiles)

        def place(o, carry):
            b = o // tiles
            key = b * (tiles * nx) + o - b * tiles
            total = jnp.zeros((rows, tile), jnp.float32) if chain == 0 else acc[o]
            for n, found in enumerate(keys):
                total = total + prod[n] * jnp.where(found == key, 1.0, 0.0).astype(jnp.float32)
            acc[o] = total
            return carry

        lax.fori_loop(0, width * tiles, place, 0)

    def denominators():
        for copy in own_en:
            copy.wait()
        column = jnp.transpose(jnp.broadcast_to(gap[...], (rows, tile)))
        for b in range(width):
            for t in range(tiles):
                inv[b * tiles + t] = 1.0 / (win[0, b] + column + vir[t : t + 1, :])

    second = {}

    def hole(b, d):
        if b not in state["own"]:
            own_x[b].wait()
            for e in far_first:
                first[b, e].wait_recv()
            state["own"].add(b)
        if not state["h"]:
            own_h.wait()
            state["h"] = True
        to = lax.rem(y + d, ny)
        value = jnp.dot(hv[span(to, rows), :], x_in[b], preferred_element_type=jnp.float32)
        if d == 0:
            yown[b] = value
            return
        top = jnp.maximum(jnp.max(jnp.abs(value), axis=0, keepdims=True), LEAST)
        code = jnp.floor(value * (LEVELS / top) + 0.5)
        ysend[b, d] = code.astype(jnp.int32).astype(jnp.int16)
        ssend[b, d] = jnp.broadcast_to(top * (1.0 / LEVELS), ssend.shape[2:])
        second[b, d] = [
            remote(ysend.at[b, d], yrecv.at[b, d], y2_ss.at[0, b, d], y2_rs.at[0, b, d], ypeer(d)),
            remote(ssend.at[b, d], srecv.at[b, d], y2_ss.at[1, b, d], y2_rs.at[1, b, d], ypeer(d)),
        ]
        for copy in second[b, d]:
            send(copy)

    def finish(b, d):
        col = lax.rem(y - d + ny, ny)
        if d == 0:
            value = yown[b]
        else:
            for copy in second[b, d]:
                copy.wait_recv()
            value = yrecv[b, d].astype(jnp.int32).astype(jnp.float32) * srecv[b, d, 0:1, :]
        out_ref[b, :, span(col, tile)] = (acc[b * tiles + col] + value) * inv[b * tiles + col]

    step = 0.65 * CHUNK
    events = []
    ends = {}
    for n, (tick, direction, chain, hop) in enumerate(z_order(nz, chains)):
        when = 2.5 + step * tick
        events.append((when, n, functools.partial(z_message, direction, chain, hop)))
        if hop == hops(direction, chain, nz) - 1:
            ends[chain] = max(ends.get(chain, 0.0), when)
    for chain in range(chains):
        events.append((ends[chain] + step + 1.5, 1000 + chain, functools.partial(z_final, chain)))
        events.append((ends[chain] + 2 * step + 4.5, 2000 + chain, functools.partial(products, chain)))
    for b in range(width):
        for n, d in enumerate(far_first + [0]):
            events.append((7.5 + 5.3 * b + 0.5 * n, 3000 + n, functools.partial(hole, b, d)))
    events.append((5.0, 5000, denominators))
    for b in range(width):
        for n, d in enumerate([0] + far_first):
            events.append((100.0 + b, 4000 + n, functools.partial(finish, b, d)))
    for _, _, event in sorted(events, key=lambda e: e[:2]):
        event()
    for copy in sends:
        copy.wait_send()


def local(
    amplitudes,
    pp_blocks,
    src_tiles,
    src_wins,
    dst_tiles,
    dst_wins,
    hh_integrals,
    pair_gap,
    vir_energy,
    win_energy,
):
    ny = lax.axis_size("amp")
    nz = lax.axis_size("int") // 2
    nx = lax.axis_size("rep")
    width, rows, ncol = amplitudes.shape
    tile = pp_blocks.shape[-1]
    slots = pp_blocks.shape[1]
    tiles = ncol // tile
    chains = slots // CHUNK
    bf, f32, i32 = jnp.bfloat16, jnp.float32, jnp.int32
    dma = pltpu.SemaphoreType.DMA
    vmem = pl.BlockSpec(memory_space=pltpu.VMEM)
    hbm = pl.BlockSpec(memory_space=pltpu.HBM)
    return pl.pallas_call(
        functools.partial(kernel, ny, nz, nx, chains),
        out_shape=jax.ShapeDtypeStruct((width, rows, ncol), f32),
        in_specs=[hbm] * 10,
        out_specs=vmem,
        scratch_shapes=[
            pltpu.VMEM((4, 1, slots), i32),
            pltpu.VMEM((1, rows), f32),
            pltpu.VMEM((tiles, tile), f32),
            pltpu.SMEM((1, width), f32),
            pltpu.VMEM((width * tiles, rows, tile), f32),
            pltpu.VMEM((tiles, 2 * width, rows, tile), bf),
            pltpu.VMEM((width, ny * rows, tile), bf),
            pltpu.VMEM(hh_integrals.shape, bf),
            pltpu.VMEM((nx, slots, tile, tile), bf),
            pltpu.VMEM((nx, slots, rows, tile), bf),
            pltpu.VMEM((2, chains, CHUNK, rows, tile), bf),
            pltpu.VMEM((2, chains, nz // 2, CHUNK, rows, tile), bf),
            pltpu.VMEM((nz + nx, 8, 128), i32),
            pltpu.SMEM((nz + nx, 8, 128), i32),
            pltpu.VMEM((width, ny, rows, tile), jnp.int16),
            pltpu.VMEM((width, ny, 8, tile), f32),
            pltpu.VMEM((width, ny, rows, tile), jnp.int16),
            pltpu.VMEM((width, ny, 8, tile), f32),
            pltpu.VMEM((width, rows, tile), f32),
            pltpu.VMEM((width * tiles, rows, tile), f32),
            pltpu.VMEM((nx * CHUNK, rows, tile), f32),
            dma((7,)),
            dma((tiles,)),
            dma((8,)),
            dma((2, tiles)),
            dma((nz + nx,)),
            dma((nz + nx,)),
            dma((width, ny)),
            dma((width, ny)),
            dma((2, width, ny)),
            dma((2, width, ny)),
            dma((2, chains, nz // 2)),
            dma((2, chains, nz // 2)),
            dma((nx,)),
            dma((nx,)),
            dma((chains, nx)),
            dma((chains, nx)),
        ],
        compiler_params=pltpu.CompilerParams(
            collective_id=0, has_side_effects=True, vmem_limit_bytes=40 * 1024 * 1024
        ),
        cost_estimate=pl.CostEstimate(flops=700_000_000, bytes_accessed=5_000_000, transcendentals=0),
        name="ladder",
    )(
        src_tiles, src_wins, dst_tiles, dst_wins, amplitudes, pp_blocks, hh_integrals,
        pair_gap.reshape(1, rows), vir_energy.reshape(tiles, tile), win_energy.reshape(1, width),
    )


def solution(mesh):
    placed = (
        P("int", "amp", "rep"),
        P("rep", "int", None, None),
        P("rep", "int"),
        P("rep", "int"),
        P("rep", "int"),
        P("rep", "int"),
        P(),
        P("amp"),
        P("rep"),
        P("int"),
    )
    return jax.shard_map(
        local, mesh=mesh, in_specs=placed, out_specs=P("int", "amp", "rep"), check_vma=False
    )
```

```python
import functools

import jax
import jax.numpy as jnp
from jax import lax
from jax.experimental import pallas as pl
from jax.experimental.pallas import tpu as pltpu
from jax.sharding import PartitionSpec as P

MESH = pl.DeviceIdType.MESH
CHUNK = 1
LEVELS = 32760.0
LEAST = 1e-33
SLAB, DUE, APART, HOP, DELAY, SHARE, SHARE_DELAY = 0.65, 9.75, 1.95, 3.9, 1.5, 1.3, 1.8
START, COST_Z, COST_F, COST_P, COST_H = 5.0, 0.12, 0.2, 0.7, 0.45


def hops(direction, chain, nz):
    return nz // 2 - ((chain + direction) % 2)


def plan(nz, chains, width, ny):
    slab, share = SLAB * CHUNK, SHARE * CHUNK
    todo = {}
    for j in range(chains):
        due = DUE + APART * j * CHUNK
        for d in (0, 1):
            for h in range(hops(d, j, nz)):
                todo["z", d, j, h] = due - (hops(d, j, nz) - 1 - h) * HOP
        todo["f", j] = due + DELAY
        todo["p", j] = due + DELAY + 6.0
    landed = [2.0 + (b + 1) * ny * SLAB + DELAY for b in range(width)]
    for b in range(width):
        for n in range(ny):
            todo["h", b, n] = landed[b] + n * SLAB
    now, zfree, xfree, arrive, order = 0.0, [0.0, 0.0], 0.0, {}, []

    def ready(k):
        if k[0] == "z":
            return START if k[3] == 0 else arrive.get(("z", k[1], k[2], k[3] - 1), 1e9)
        if k[0] == "f":
            return max(arrive.get(("z", d, k[1], hops(d, k[1], nz) - 1), 1e9) for d in (0, 1))
        return landed[k[1]] if k[0] == "h" else arrive.get(k, 1e9)

    while todo:
        when = {k: ready(k) for k in todo}
        open_now = [k for k in todo if when[k] <= now]
        if not open_now:
            now = min(when.values())
            continue
        k = min(open_now, key=lambda k: (todo[k], k))
        del todo[k]
        order.append(k)
        if k[0] == "z":
            now += COST_Z
            zfree[k[1]] = max(now, zfree[k[1]]) + slab
            arrive[k] = zfree[k[1]] + DELAY
        elif k[0] == "f":
            now += COST_F
            xfree = max(now, xfree) + share
            arrive["p", k[1]] = xfree + SHARE_DELAY
        else:
            now += COST_P if k[0] == "p" else COST_H
    return order


def kernel(
    ny, nz, nx, chains,
    st_ref, sw_ref, dt_ref, dw_ref, amp_ref, blk_ref, h_ref, gap_ref, vir_ref, win_ref,
    out_ref,
    gap, vir, win, inv, achip, x_in, hv, ball, sall, zinj, zbuf, idxs, ysend, ssend, yrecv, srecv, yown, acc, prod,
    tab_sem, amp_sem, loc_sem, sib_sem, idx_ss, idx_rs, y1_ss, y1_rs, y2_ss, y2_rs, z_ss, z_rs, b_ss, b_rs, s_ss, s_rs,
):
    width, rows, ncol = amp_ref.shape
    tile = blk_ref.shape[-1]
    tiles = ncol // tile
    per_chip = 2 * width
    slots = blk_ref.shape[1]
    y = lax.axis_index("amp")
    i = lax.axis_index("int")
    x = lax.axis_index("rep")
    z = i // 2
    core = lax.rem(i, 2)

    def ypeer(d):
        return {"amp": lax.rem(y + (d + ny) % ny, ny)}

    def zpeer(d):
        return {"int": lax.rem(i + 2 * ((d + nz) % nz), 2 * nz)}

    def xpeer(d):
        return {"rep": lax.rem(x + (d + nx) % nx, nx)}

    sibling = {"int": i + 1 - 2 * core}
    peers = [ypeer(d) for d in range(1, ny)] + [zpeer(d) for d in range(1, nz)]
    peers += [xpeer(d) for d in range(1, nx)] + [sibling]

    def remote(src, dst, ss, rs, peer):
        return pltpu.make_async_remote_copy(
            src_ref=src, dst_ref=dst, send_sem=ss, recv_sem=rs, device_id=peer, device_id_type=MESH
        )

    def span(index, size):
        return pl.ds(pl.multiple_of(index * size, size), size)

    sends = []

    def send(copy):
        copy.start()
        sends.append(copy)

    barrier = pltpu.get_barrier_semaphore()
    for peer in peers:
        pl.semaphore_signal(barrier, inc=1, device_id=peer, device_id_type=MESH)

    lists = (st_ref, sw_ref, dt_ref, dw_ref)
    own_tab = [
        pltpu.make_async_copy(ref, idxs.at[place, n % 2], tab_sem.at[n])
        for n, (ref, place) in enumerate(zip(lists, (z, z, nz + x, nz + x)))
    ]
    own_en = [
        pltpu.make_async_copy(ref, to, tab_sem.at[4 + n])
        for n, (ref, to) in enumerate(((gap_ref, gap), (vir_ref, vir), (win_ref, win)))
    ]
    own_amp = [
        pltpu.make_async_copy(
            amp_ref.at[:, :, t * tile : (t + 1) * tile], achip.at[t, pl.ds(core * width, width)], amp_sem.at[t]
        )
        for t in range(tiles)
    ]
    own_h = pltpu.make_async_copy(h_ref, hv, loc_sem.at[1])
    own_blk = pltpu.make_async_copy(blk_ref.at[0], ball.at[x], loc_sem.at[2])
    own_x = [
        pltpu.make_async_copy(
            amp_ref.at[b, :, span(y, tile)], x_in.at[b, span(y, rows), :], loc_sem.at[3 + b]
        )
        for b in range(width)
    ]
    for copy in own_tab + own_x + own_amp + [own_h, own_blk] + own_en:
        copy.start()
    pl.semaphore_wait(barrier, len(peers))

    far_z = sorted(range(1, nz), key=lambda d: -min(d, nz - d))
    idx_z = [
        remote(lists[n], idxs.at[z, n], idx_ss.at[n, d], idx_rs.at[n, d], zpeer(d)) for d in far_z for n in (0, 1)
    ]
    idx_x = [
        remote(lists[2 + n], idxs.at[nz + x, n], idx_ss.at[n, nz + d], idx_rs.at[n, nz + d], xpeer(d))
        for d in range(1, nx)
        for n in (0, 1)
    ]
    for copy in idx_z:
        send(copy)
    twin = []
    for t in range(tiles):
        part = achip.at[t, pl.ds(core * width, width)]
        twin.append(
            remote(amp_ref.at[:, :, t * tile : (t + 1) * tile], part, sib_sem.at[0, t], sib_sem.at[1, t], sibling)
        )
        send(twin[t])
    far_first = sorted(range(1, ny), key=lambda d: -min(d, ny - d))
    first = {}
    for b in range(width):
        for d in far_first:
            to = lax.rem(y + d, ny)
            first[b, d] = remote(
                amp_ref.at[b, :, span(to, tile)],
                x_in.at[b, span(y, rows), :],
                y1_ss.at[b, d],
                y1_rs.at[b, d],
                ypeer(d),
            )
            send(first[b, d])
    for copy in idx_x:
        send(copy)
    shared = [remote(blk_ref.at[0], ball.at[x], b_ss.at[d], b_rs.at[d], xpeer(d)) for d in range(1, nx)]
    for copy in shared:
        send(copy)

    for copy in idx_z:
        copy.wait_recv()
    for copy in own_tab:
        copy.wait()
    for t in range(tiles):
        own_amp[t].wait()
        twin[t].wait_recv()

    def slab(place, slot):
        win = idxs[place, 1, 0, slot]
        col = idxs[place, 0, 0, slot]
        return lax.div(win, per_chip), achip[col, lax.rem(win, per_chip)]

    moves = {}

    def z_message(direction, chain, hop):
        far = hops(direction, chain, nz)
        sign = 1 - 2 * direction
        dest = lax.rem(z + (sign * (far - hop) + nz) % nz, nz)
        if hop == 0:
            buf = zinj.at[direction, chain]
        else:
            buf = zbuf.at[direction, chain, hop - 1]
            moves[direction, chain, hop - 1].wait_recv()
        for k in range(CHUNK):
            owner, value = slab(dest, chain * CHUNK + k)
            if hop > 0:
                value = jnp.where(owner == z, value, buf[k])
            buf[k] = value
        moves[direction, chain, hop] = remote(
            buf,
            zbuf.at[direction, chain, hop],
            z_ss.at[direction, chain, hop],
            z_rs.at[direction, chain, hop],
            zpeer(sign),
        )
        send(moves[direction, chain, hop])

    spread = {}

    def z_final(chain):
        last = [hops(direction, chain, nz) for direction in (0, 1)]
        for direction in (0, 1):
            moves[direction, chain, last[direction] - 1].wait_recv()
        for k in range(CHUNK):
            slot = chain * CHUNK + k
            owner, value = slab(z, slot)
            behind = lax.rem(z - owner + nz, nz)
            up = zbuf[0, chain, last[0] - 1, k]
            down = zbuf[1, chain, last[1] - 1, k]
            value = jnp.where(owner == z, value, jnp.where(behind <= last[0], up, down))
            sall[x, slot] = value
        part = sall.at[x, pl.ds(chain * CHUNK, CHUNK)]
        for d in (list(range(2, nx)) + [1]):
            spread[chain, d] = remote(part, part, s_ss.at[chain, d], s_rs.at[chain, d], xpeer(d))
            send(spread[chain, d])

    state = {"blocks": False, "own": set(), "h": False}

    def products(chain):
        fresh = not state["blocks"]
        if not state["blocks"]:
            own_blk.wait()
            for copy in idx_x + shared:
                copy.wait_recv()
            state["blocks"] = True
        keys = []
        for d in range(nx):
            origin = lax.rem(x - d + nx, nx)
            if d > 0:
                spread[chain, d].wait_recv()
            for k in range(CHUNK):
                slot = chain * CHUNK + k
                prod[d * CHUNK + k] = jnp.dot(
                    sall[origin, slot], ball[origin, slot], preferred_element_type=jnp.float32
                )
                keys.append(idxs[nz + origin, 1, 0, slot] * (tiles * nx) + idxs[nz + origin, 0, 0, slot] - x * tiles)

        def place(o, carry):
            b = o // tiles
            key = b * (tiles * nx) + o - b * tiles
            total = jnp.zeros((rows, tile), jnp.float32) if fresh else acc[o]
            for n, found in enumerate(keys):
                total = total + prod[n] * jnp.where(found == key, 1.0, 0.0).astype(jnp.float32)
            acc[o] = total
            return carry

        lax.fori_loop(0, width * tiles, place, 0)

    def denominators():
        for copy in own_en:
            copy.wait()
        column = jnp.transpose(jnp.broadcast_to(gap[...], (rows, tile)))
        for b in range(width):
            for t in range(tiles):
                inv[b * tiles + t] = 1.0 / (win[0, b] + column + vir[t : t + 1, :])

    second = {}

    def hole(b, d):
        if b not in state["own"]:
            own_x[b].wait()
            for e in far_first:
                first[b, e].wait_recv()
            state["own"].add(b)
        if not state["h"]:
            own_h.wait()
            state["h"] = True
        to = lax.rem(y + d, ny)
        value = jnp.dot(hv[span(to, rows), :], x_in[b], preferred_element_type=jnp.float32)
        if d == 0:
            yown[b] = value
            return
        top = jnp.maximum(jnp.max(jnp.abs(value), axis=0, keepdims=True), LEAST)
        code = jnp.floor(value * (LEVELS / top) + 0.5)
        ysend[b, d] = code.astype(jnp.int32).astype(jnp.int16)
        ssend[b, d] = jnp.broadcast_to(top * (1.0 / LEVELS), ssend.shape[2:])
        second[b, d] = [
            remote(ysend.at[b, d], yrecv.at[b, d], y2_ss.at[0, b, d], y2_rs.at[0, b, d], ypeer(d)),
            remote(ssend.at[b, d], srecv.at[b, d], y2_ss.at[1, b, d], y2_rs.at[1, b, d], ypeer(d)),
        ]
        for copy in second[b, d]:
            send(copy)

    def finish(b, d):
        col = lax.rem(y - d + ny, ny)
        if d == 0:
            value = yown[b]
        else:
            for copy in second[b, d]:
                copy.wait_recv()
            value = yrecv[b, d].astype(jnp.int32).astype(jnp.float32) * srecv[b, d, 0:1, :]
        out_ref[b, :, span(col, tile)] = (acc[b * tiles + col] + value) * inv[b * tiles + col]

    runs = {"z": z_message, "f": z_final, "p": products, "h": lambda b, n: hole(b, (far_first + [0])[n])}
    for n, (kind, *place) in enumerate(plan(nz, chains, width, ny)):
        runs[kind](*place)
        if n == 2 * chains:
            denominators()
    for b in range(width):
        for d in [0] + far_first:
            finish(b, d)
    for copy in sends:
        copy.wait_send()


def local(
    amplitudes,
    pp_blocks,
    src_tiles,
    src_wins,
    dst_tiles,
    dst_wins,
    hh_integrals,
    pair_gap,
    vir_energy,
    win_energy,
):
    ny = lax.axis_size("amp")
    nz = lax.axis_size("int") // 2
    nx = lax.axis_size("rep")
    width, rows, ncol = amplitudes.shape
    tile = pp_blocks.shape[-1]
    slots = pp_blocks.shape[1]
    tiles = ncol // tile
    chains = slots // CHUNK
    bf, f32, i32 = jnp.bfloat16, jnp.float32, jnp.int32
    dma = pltpu.SemaphoreType.DMA
    vmem = pl.BlockSpec(memory_space=pltpu.VMEM)
    hbm = pl.BlockSpec(memory_space=pltpu.HBM)
    return pl.pallas_call(
        functools.partial(kernel, ny, nz, nx, chains),
        out_shape=jax.ShapeDtypeStruct((width, rows, ncol), f32),
        in_specs=[hbm] * 10,
        out_specs=vmem,
        scratch_shapes=[
            pltpu.VMEM((1, rows), f32),
            pltpu.VMEM((tiles, tile), f32),
            pltpu.SMEM((1, width), f32),
            pltpu.VMEM((width * tiles, rows, tile), f32),
            pltpu.VMEM((tiles, 2 * width, rows, tile), bf),
            pltpu.VMEM((width, ny * rows, tile), bf),
            pltpu.VMEM(hh_integrals.shape, bf),
            pltpu.VMEM((nx, slots, tile, tile), bf),
            pltpu.VMEM((nx, slots, rows, tile), bf),
            pltpu.VMEM((2, chains, CHUNK, rows, tile), bf),
            pltpu.VMEM((2, chains, nz // 2, CHUNK, rows, tile), bf),
            pltpu.SMEM((nz + nx, 2, 1, slots), i32),
            pltpu.VMEM((width, ny, rows, tile), jnp.int16),
            pltpu.VMEM((width, ny, 8, tile), f32),
            pltpu.VMEM((width, ny, rows, tile), jnp.int16),
            pltpu.VMEM((width, ny, 8, tile), f32),
            pltpu.VMEM((width, rows, tile), f32),
            pltpu.VMEM((width * tiles, rows, tile), f32),
            pltpu.VMEM((nx * CHUNK, rows, tile), f32),
            dma((7,)),
            dma((tiles,)),
            dma((8,)),
            dma((2, tiles)),
            dma((2, nz + nx)),
            dma((2, nz + nx)),
            dma((width, ny)),
            dma((width, ny)),
            dma((2, width, ny)),
            dma((2, width, ny)),
            dma((2, chains, nz // 2)),
            dma((2, chains, nz // 2)),
            dma((nx,)),
            dma((nx,)),
            dma((chains, nx)),
            dma((chains, nx)),
        ],
        compiler_params=pltpu.CompilerParams(
            collective_id=0, has_side_effects=True, vmem_limit_bytes=60 * 1024 * 1024
        ),
        cost_estimate=pl.CostEstimate(flops=700_000_000, bytes_accessed=5_000_000, transcendentals=0),
        name="ladder",
    )(
        src_tiles, src_wins, dst_tiles, dst_wins, amplitudes, pp_blocks, hh_integrals,
        pair_gap.reshape(1, rows), vir_energy.reshape(tiles, tile), win_energy.reshape(1, width),
    )


def solution(mesh):
    placed = (
        P("int", "amp", "rep"),
        P("rep", "int", None, None),
        P("rep", "int"),
        P("rep", "int"),
        P("rep", "int"),
        P("rep", "int"),
        P(),
        P("amp"),
        P("rep"),
        P("int"),
    )
    return jax.shard_map(
        local, mesh=mesh, in_specs=placed, out_specs=P("int", "amp", "rep"), check_vma=False
    )
```

```python
import functools

import jax
import jax.numpy as jnp
from jax import lax
from jax.experimental import pallas as pl
from jax.experimental.pallas import tpu as pltpu
from jax.sharding import PartitionSpec as P

MESH = pl.DeviceIdType.MESH
CHUNK = 1
LEVELS = 32760.0
LEAST = 1e-33
SLAB, DUE, APART, DELAY = 0.66, 6.0, 0.6, 2.3
START, COST_Z, COST_F, COST_H = 5.0, 0.12, 0.2, 0.45
POWER = 0.85
WINDOW = 4


def hops(direction, chain, nz):
    return nz // 2 - ((chain + direction) % 2)


def plan(nz, chains, width, ny):
    slab = SLAB * CHUNK
    todo = {}
    for j in range(chains):
        due = DUE + APART * j * CHUNK
        for d in (0, 1):
            far = hops(d, j, nz)
            for h in range(far):
                todo["z", d, j, h] = START + due * (2 * (h + 1 + nz // 2 - far) / nz) ** POWER
        todo["f", j] = START + due + DELAY
    landed = [2.0 + (b + 1) * ny * SLAB + DELAY for b in range(width)]
    for b in range(width):
        for n in range(ny):
            todo["h", b, n] = landed[b] + n * SLAB
    now, zfree, arrive, order = 0.0, [0.0, 0.0], {}, []

    def ready(k):
        if k[0] == "z":
            here = START if k[3] == 0 else arrive.get(("z", k[1], k[2], k[3] - 1), 1e9)
            return max(here, zfree[k[1]] - slab)
        if k[0] == "f":
            return max(arrive.get(("z", d, k[1], hops(d, k[1], nz) - 1), 1e9) for d in (0, 1))
        return landed[k[1]]

    while todo:
        when = {k: ready(k) for k in todo}
        open_now = [k for k in todo if when[k] <= now]
        if not open_now:
            now = min(when.values())
            continue
        k = min(open_now, key=lambda k: (todo[k], k))
        del todo[k]
        order.append(k)
        if k[0] == "z":
            now += COST_Z
            zfree[k[1]] = max(now, zfree[k[1]]) + slab
            arrive[k] = zfree[k[1]] + DELAY
        elif k[0] == "f":
            now += COST_F
        else:
            now += COST_H
    return order


def kernel(
    ny, nz, nx, chains,
    st_ref, sw_ref, dt_ref, dw_ref, amp_ref, blk_ref, h_ref,
    s_out, b_out, y_out, r_out, i_out,
    achip, x_in, hv, sall, zinj, zbuf, idxs, ysend, ssend,
    tab_sem, amp_sem, loc_sem, own_sem, sib_sem, idx_ss, idx_rs, y1_ss, y1_rs, y2_ss, y2_rs, z_ss, z_rs, b_ss, b_rs, s_ss, s_rs,
):
    width, rows, ncol = amp_ref.shape
    tile = blk_ref.shape[-1]
    tiles = ncol // tile
    per_chip = 2 * width
    slots = blk_ref.shape[1]
    y = lax.axis_index("amp")
    i = lax.axis_index("int")
    x = lax.axis_index("rep")
    z = i // 2
    core = lax.rem(i, 2)

    def ypeer(d):
        return {"amp": lax.rem(y + (d + ny) % ny, ny)}

    def zpeer(d):
        return {"int": lax.rem(i + 2 * ((d + nz) % nz), 2 * nz)}

    def xpeer(d):
        return {"rep": lax.rem(x + (d + nx) % nx, nx)}

    sibling = {"int": i + 1 - 2 * core}
    peers = [ypeer(d) for d in range(1, ny)] + [zpeer(d) for d in range(1, nz)]
    peers += [xpeer(d) for d in range(1, nx)] + [sibling]

    def remote(src, dst, ss, rs, peer):
        return pltpu.make_async_remote_copy(
            src_ref=src, dst_ref=dst, send_sem=ss, recv_sem=rs, device_id=peer, device_id_type=MESH
        )

    def span(index, size):
        return pl.ds(pl.multiple_of(index * size, size), size)

    sends = []

    kept = []

    def keep(copy):
        copy.start()
        kept.append(copy)

    def send(copy):
        copy.start()
        sends.append(copy)

    barrier = pltpu.get_barrier_semaphore()
    for peer in peers:
        pl.semaphore_signal(barrier, inc=1, device_id=peer, device_id_type=MESH)

    lists = (st_ref, sw_ref, dt_ref, dw_ref)
    own_tab = [
        pltpu.make_async_copy(ref, to, tab_sem.at[n])
        for n, (ref, to) in enumerate(zip(lists, (idxs.at[z, 0], idxs.at[z, 1], i_out.at[x, 0], i_out.at[x, 1])))
    ]
    own_amp = [
        pltpu.make_async_copy(
            amp_ref.at[:, :, t * tile : (t + 1) * tile], achip.at[t, pl.ds(core * width, width)], amp_sem.at[t]
        )
        for t in range(tiles)
    ]
    own_h = pltpu.make_async_copy(h_ref, hv, loc_sem.at[1])
    own_blk = pltpu.make_async_copy(blk_ref.at[0], b_out.at[x], loc_sem.at[2])
    own_x = [
        pltpu.make_async_copy(
            amp_ref.at[b, :, span(y, tile)], x_in.at[b, span(y, rows), :], loc_sem.at[3 + b]
        )
        for b in range(width)
    ]
    for copy in own_tab + own_x + own_amp + [own_h, own_blk]:
        copy.start()
    pl.semaphore_wait(barrier, len(peers))

    far_z = sorted(range(1, nz), key=lambda d: -min(d, nz - d))
    idx_z = [
        remote(lists[n], idxs.at[z, n], idx_ss.at[n, d], idx_rs.at[n, d], zpeer(d)) for d in far_z for n in (0, 1)
    ]
    idx_x = [
        remote(lists[2 + n], i_out.at[x, n], idx_ss.at[n, nz + d], idx_rs.at[n, nz + d], xpeer(d))
        for d in range(1, nx)
        for n in (0, 1)
    ]
    for copy in idx_z:
        send(copy)
    twin = []
    for t in range(tiles):
        part = achip.at[t, pl.ds(core * width, width)]
        twin.append(
            remote(amp_ref.at[:, :, t * tile : (t + 1) * tile], part, sib_sem.at[0, t], sib_sem.at[1, t], sibling)
        )
        send(twin[t])
    far_first = sorted(range(1, ny), key=lambda d: -min(d, ny - d))
    first = {}
    for b in range(width):
        for d in far_first:
            to = lax.rem(y + d, ny)
            first[b, d] = remote(
                amp_ref.at[b, :, span(to, tile)],
                x_in.at[b, span(y, rows), :],
                y1_ss.at[b, d],
                y1_rs.at[b, d],
                ypeer(d),
            )
            send(first[b, d])
    for copy in idx_x:
        send(copy)
    shared = [remote(blk_ref.at[0], b_out.at[x], b_ss.at[d], b_rs.at[d], xpeer(d)) for d in range(1, nx)]
    for copy in shared:
        send(copy)

    for copy in idx_z:
        copy.wait_recv()
    for copy in own_tab[:2]:
        copy.wait()
    for t in range(tiles):
        own_amp[t].wait()
        twin[t].wait_recv()

    def slab(place, slot):
        win = idxs[place, 1, 0, slot]
        col = idxs[place, 0, 0, slot]
        return lax.div(win, per_chip), achip[col, lax.rem(win, per_chip)]

    moves = {}
    flying = [[], []]

    def z_message(direction, chain, hop):
        far = hops(direction, chain, nz)
        sign = 1 - 2 * direction
        dest = lax.rem(z + (sign * (far - hop) + nz) % nz, nz)
        if hop == 0:
            buf = zinj.at[direction, chain]
        else:
            buf = zbuf.at[direction, chain, hop - 1]
            moves[direction, chain, hop - 1].wait_recv()
        if len(flying[direction]) == WINDOW:
            flying[direction].pop(0).wait_send()
        for k in range(CHUNK):
            owner, value = slab(dest, chain * CHUNK + k)
            if hop > 0:
                value = jnp.where(owner == z, value, buf[k])
            buf[k] = value
        moves[direction, chain, hop] = remote(
            buf,
            zbuf.at[direction, chain, hop],
            z_ss.at[direction, chain, hop],
            z_rs.at[direction, chain, hop],
            zpeer(sign),
        )
        flying[direction].append(moves[direction, chain, hop])
        flying[direction][-1].start()

    spread = {}

    def z_final(chain):
        last = [hops(direction, chain, nz) for direction in (0, 1)]
        for direction in (0, 1):
            moves[direction, chain, last[direction] - 1].wait_recv()
        for k in range(CHUNK):
            slot = chain * CHUNK + k
            owner, value = slab(z, slot)
            behind = lax.rem(z - owner + nz, nz)
            up = zbuf[0, chain, last[0] - 1, k]
            down = zbuf[1, chain, last[1] - 1, k]
            value = jnp.where(owner == z, value, jnp.where(behind <= last[0], up, down))
            sall[slot] = value
        part = sall.at[pl.ds(chain * CHUNK, CHUNK)]
        to = s_out.at[x, pl.ds(chain * CHUNK, CHUNK)]
        for d in (list(range(2, nx)) + [1]):
            spread[chain, d] = remote(part, to, s_ss.at[chain, d], s_rs.at[chain, d], xpeer(d))
            send(spread[chain, d])
        keep(pltpu.make_async_copy(part, to, own_sem.at[chain]))

    state = {"own": set(), "h": False}

    second = {}

    def hole(b, d):
        if b not in state["own"]:
            own_x[b].wait()
            for e in far_first:
                first[b, e].wait_recv()
            state["own"].add(b)
        if not state["h"]:
            own_h.wait()
            state["h"] = True
        to = lax.rem(y + d, ny)
        value = jnp.dot(hv[span(to, rows), :], x_in[b], preferred_element_type=jnp.float32)
        top = jnp.maximum(jnp.max(jnp.abs(value), axis=0, keepdims=True), LEAST)
        code = jnp.floor(value * (LEVELS / top) + 0.5)
        ysend[b, d] = code.astype(jnp.int32).astype(jnp.int16)
        ssend[b, d] = jnp.broadcast_to(top * (1.0 / LEVELS), ssend.shape[2:])
        pairs = ((ysend.at[b, d], y_out.at[b, y]), (ssend.at[b, d], r_out.at[b, y]))
        if d == 0:
            for n, (here, there) in enumerate(pairs):
                keep(pltpu.make_async_copy(here, there, own_sem.at[chains + 2 * b + n]))
            return
        second[b, d] = [
            remote(here, there, y2_ss.at[n, b, d], y2_rs.at[n, b, d], ypeer(d))
            for n, (here, there) in enumerate(pairs)
        ]
        for copy in second[b, d]:
            send(copy)

    runs = {"z": z_message, "f": z_final, "h": lambda b, n: hole(b, (far_first + [0])[n])}
    for kind, *place in plan(nz, chains, width, ny):
        runs[kind](*place)
    own_blk.wait()
    for copy in own_tab[2:] + kept:
        copy.wait()
    for copy in idx_x + shared + list(spread.values()) + [copy for pair in second.values() for copy in pair]:
        copy.wait_recv()
    for copy in sends + flying[0] + flying[1]:
        copy.wait_send()


def finish(idx, win, s_ref, b_ref, y_ref, r_ref, gap_ref, vir_ref, out_ref, s, b, y, r, gap, vir, acc, out, sem):
    origins, slots, rows, tile = s.shape
    width, tiles = y.shape[:2]
    x = lax.axis_index("rep")
    first = [
        pltpu.make_async_copy(here, there, sem.at[n])
        for n, (here, there) in enumerate(((gap_ref, gap), (vir_ref, vir), (y_ref, y), (r_ref, r)))
    ]
    blocks = [
        [
            pltpu.make_async_copy(s_ref.at[o], s.at[o], sem.at[4 + 2 * o]),
            pltpu.make_async_copy(b_ref.at[o], b.at[o], sem.at[5 + 2 * o]),
        ]
        for o in range(origins)
    ]
    for copy in first + [copy for pair in blocks for copy in pair]:
        copy.start()
    for o in range(width * tiles + 1):
        acc[o] = jnp.zeros((rows, tile), jnp.float32)
    for o in range(origins):
        for copy in blocks[o]:
            copy.wait()
        for k in range(slots):
            place = idx[o, 1, 0, k] * tiles + idx[o, 0, 0, k] - x * tiles
            inside = (idx[o, 0, 0, k] >= x * tiles) & (idx[o, 0, 0, k] < (x + 1) * tiles)
            place = jnp.where(inside, place, width * tiles)
            acc[place] += jnp.dot(s[o, k], b[o, k], preferred_element_type=jnp.float32)
    for copy in first:
        copy.wait()
    column = jnp.transpose(jnp.broadcast_to(gap[...], (rows, tile)))
    done = []
    for n in range(width):
        for t in range(tiles):
            value = y[n, t].astype(jnp.int32).astype(jnp.float32) * r[n, t, 0:1, :] + acc[n * tiles + t]
            out[n, :, t * tile : (t + 1) * tile] = value / (win[0, n] + column + vir[t : t + 1, :])
        done.append(pltpu.make_async_copy(out.at[n], out_ref.at[n], sem.at[4 + 2 * origins + n]))
        done[n].start()
    for copy in done:
        copy.wait()


def local(
    amplitudes,
    pp_blocks,
    src_tiles,
    src_wins,
    dst_tiles,
    dst_wins,
    hh_integrals,
    pair_gap,
    vir_energy,
    win_energy,
):
    ny = lax.axis_size("amp")
    nz = lax.axis_size("int") // 2
    nx = lax.axis_size("rep")
    width, rows, ncol = amplitudes.shape
    tile = pp_blocks.shape[-1]
    slots = pp_blocks.shape[1]
    tiles = ncol // tile
    chains = slots // CHUNK
    bf, f32, i32 = jnp.bfloat16, jnp.float32, jnp.int32
    dma = pltpu.SemaphoreType.DMA
    hbm = pl.BlockSpec(memory_space=pltpu.HBM)
    smem = pl.BlockSpec(memory_space=pltpu.SMEM)
    slabs, blocks, codes, scales, places = pl.pallas_call(
        functools.partial(kernel, ny, nz, nx, chains),
        out_shape=[
            jax.ShapeDtypeStruct((nx, slots, rows, tile), bf),
            jax.ShapeDtypeStruct((nx, slots, tile, tile), bf),
            jax.ShapeDtypeStruct((width, ny, rows, tile), jnp.int16),
            jax.ShapeDtypeStruct((width, ny, 8, tile), f32),
            jax.ShapeDtypeStruct((nx, 2, 1, slots), i32),
        ],
        in_specs=[hbm] * 7,
        out_specs=[hbm] * 5,
        scratch_shapes=[
            pltpu.VMEM((tiles, 2 * width, rows, tile), bf),
            pltpu.VMEM((width, ny * rows, tile), bf),
            pltpu.VMEM(hh_integrals.shape, bf),
            pltpu.VMEM((slots, rows, tile), bf),
            pltpu.VMEM((2, chains, CHUNK, rows, tile), bf),
            pltpu.VMEM((2, chains, nz // 2, CHUNK, rows, tile), bf),
            pltpu.SMEM((nz, 2, 1, slots), i32),
            pltpu.VMEM((width, ny, rows, tile), jnp.int16),
            pltpu.VMEM((width, ny, 8, tile), f32),
            dma((4,)),
            dma((tiles,)),
            dma((8,)),
            dma((chains + 2 * width,)),
            dma((2, tiles)),
            dma((2, nz + nx)),
            dma((2, nz + nx)),
            dma((width, ny)),
            dma((width, ny)),
            dma((2, width, ny)),
            dma((2, width, ny)),
            dma((2, chains, nz // 2)),
            dma((2, chains, nz // 2)),
            dma((nx,)),
            dma((nx,)),
            dma((chains, nx)),
            dma((chains, nx)),
        ],
        compiler_params=pltpu.CompilerParams(
            collective_id=0, has_side_effects=True, vmem_limit_bytes=60 * 1024 * 1024
        ),
        cost_estimate=pl.CostEstimate(flops=700_000_000, bytes_accessed=5_000_000, transcendentals=0),
        name="ladder",
    )(src_tiles, src_wins, dst_tiles, dst_wins, amplitudes, pp_blocks, hh_integrals)
    return pl.pallas_call(
        finish,
        out_shape=jax.ShapeDtypeStruct((width, rows, ncol), f32),
        in_specs=[smem, smem] + [hbm] * 6,
        out_specs=hbm,
        scratch_shapes=[
            pltpu.VMEM(slabs.shape, bf),
            pltpu.VMEM(blocks.shape, bf),
            pltpu.VMEM(codes.shape, jnp.int16),
            pltpu.VMEM(scales.shape, f32),
            pltpu.VMEM((1, rows), f32),
            pltpu.VMEM((tiles, tile), f32),
            pltpu.VMEM((width * tiles + 1, rows, tile), f32),
            pltpu.VMEM((width, rows, ncol), f32),
            dma((4 + 2 * nx + width,)),
        ],
        compiler_params=pltpu.CompilerParams(vmem_limit_bytes=60 * 1024 * 1024),
        cost_estimate=pl.CostEstimate(flops=140_000_000, bytes_accessed=4_000_000, transcendentals=0),
        name="finish",
    )(
        places, win_energy.reshape(1, width), slabs, blocks, codes, scales,
        pair_gap.reshape(1, rows), vir_energy.reshape(tiles, tile),
    )


def solution(mesh):
    placed = (
        P("int", "amp", "rep"),
        P("rep", "int", None, None),
        P("rep", "int"),
        P("rep", "int"),
        P("rep", "int"),
        P("rep", "int"),
        P(),
        P("amp"),
        P("rep"),
        P("int"),
    )
    return jax.shard_map(
        local, mesh=mesh, in_specs=placed, out_specs=P("int", "amp", "rep"), check_vma=False
    )
```

```python
import functools

import jax
import jax.numpy as jnp
from jax import lax
from jax.experimental import pallas as pl
from jax.experimental.pallas import tpu as pltpu
from jax.sharding import PartitionSpec as P

MESH = pl.DeviceIdType.MESH
CHUNK = 1
LEVELS = 32760.0
LEAST = 1e-33
SLAB, DUE, APART, DELAY = 0.66, 6.0, 1.0, 2.3
START, COST_Z, COST_F, COST_H = 5.0, 0.12, 0.2, 0.45
POWER = 0.85
WINDOW = 4


def hops(direction, chain, nz):
    return nz // 2 - ((chain + direction) % 2)


def plan(nz, chains, width, ny):
    slab = SLAB * CHUNK
    todo = {}
    for j in range(chains):
        due = DUE + APART * j * CHUNK
        for d in (0, 1):
            far = hops(d, j, nz)
            for h in range(far):
                todo["z", d, j, h] = START + due * (2 * (h + 1 + nz // 2 - far) / nz) ** POWER
        todo["f", j] = START + due + DELAY
    landed = [2.0 + (b + 1) * ny * SLAB + DELAY for b in range(width)]
    for b in range(width):
        for n in range(ny):
            todo["h", b, n] = landed[b] + n * SLAB
    now, zfree, arrive, order = 0.0, [0.0, 0.0], {}, []

    def ready(k):
        if k[0] == "z":
            here = START if k[3] == 0 else arrive.get(("z", k[1], k[2], k[3] - 1), 1e9)
            return max(here, zfree[k[1]] - slab)
        if k[0] == "f":
            return max(arrive.get(("z", d, k[1], hops(d, k[1], nz) - 1), 1e9) for d in (0, 1))
        return landed[k[1]]

    while todo:
        when = {k: ready(k) for k in todo}
        open_now = [k for k in todo if when[k] <= now]
        if not open_now:
            now = min(when.values())
            continue
        k = min(open_now, key=lambda k: (todo[k], k))
        del todo[k]
        order.append(k)
        if k[0] == "z":
            now += COST_Z
            zfree[k[1]] = max(now, zfree[k[1]]) + slab
            arrive[k] = zfree[k[1]] + DELAY
        elif k[0] == "f":
            now += COST_F
        else:
            now += COST_H
    return order


def kernel(
    ny, nz, nx, chains,
    st_ref, sw_ref, dt_ref, dw_ref, amp_ref, blk_ref, h_ref,
    s_out, b_out, y_out, r_out, i_out,
    achip, x_in, hv, sall, zinj, zbuf, idxs, ysend, ssend,
    tab_sem, amp_sem, loc_sem, own_sem, sib_sem, idx_ss, idx_rs, y1_ss, y1_rs, y2_ss, y2_rs, z_ss, z_rs, b_ss, b_rs, s_ss, s_rs,
):
    width, rows, ncol = amp_ref.shape
    tile = blk_ref.shape[-1]
    tiles = ncol // tile
    per_chip = 2 * width
    slots = blk_ref.shape[1]
    y = lax.axis_index("amp")
    i = lax.axis_index("int")
    x = lax.axis_index("rep")
    z = i // 2
    core = lax.rem(i, 2)

    def ypeer(d):
        return {"amp": lax.rem(y + (d + ny) % ny, ny)}

    def zpeer(d):
        return {"int": lax.rem(i + 2 * ((d + nz) % nz), 2 * nz)}

    def xpeer(d):
        return {"rep": lax.rem(x + (d + nx) % nx, nx)}

    sibling = {"int": i + 1 - 2 * core}
    far_first = sorted(range(1, ny), key=lambda d: -min(d, ny - d))
    far_z = sorted(range(1, nz), key=lambda d: -min(d, nz - d))
    peers = [zpeer(d) for d in far_z] + [sibling] + [ypeer(d) for d in far_first]
    peers += [xpeer(d) for d in range(1, nx)]

    def remote(src, dst, ss, rs, peer):
        return pltpu.make_async_remote_copy(
            src_ref=src, dst_ref=dst, send_sem=ss, recv_sem=rs, device_id=peer, device_id_type=MESH
        )

    def span(index, size):
        return pl.ds(pl.multiple_of(index * size, size), size)

    sends = []

    kept = []

    def keep(copy):
        copy.start()
        kept.append(copy)

    def send(copy):
        copy.start()
        sends.append(copy)

    barrier = pltpu.get_barrier_semaphore()
    for peer in peers:
        pl.semaphore_signal(barrier, inc=1, device_id=peer, device_id_type=MESH)

    lists = (st_ref, sw_ref, dt_ref, dw_ref)
    own_tab = [
        pltpu.make_async_copy(ref, to, tab_sem.at[n])
        for n, (ref, to) in enumerate(zip(lists, (idxs.at[z, 0], idxs.at[z, 1], i_out.at[x, 0], i_out.at[x, 1])))
    ]
    own_amp = [
        pltpu.make_async_copy(
            amp_ref.at[:, :, t * tile : (t + 1) * tile], achip.at[t, pl.ds(core * width, width)], amp_sem.at[t]
        )
        for t in range(tiles)
    ]
    own_h = pltpu.make_async_copy(h_ref, hv, loc_sem.at[1])
    own_blk = pltpu.make_async_copy(blk_ref.at[0], b_out.at[x], loc_sem.at[2])
    own_x = [
        pltpu.make_async_copy(
            amp_ref.at[b, :, span(y, tile)], x_in.at[b, span(y, rows), :], loc_sem.at[3 + b]
        )
        for b in range(width)
    ]
    for copy in own_tab + own_x + own_amp + [own_h, own_blk]:
        copy.start()
    pl.semaphore_wait(barrier, len(peers))

    idx_z = {
        d: [remote(lists[n], idxs.at[z, n], idx_ss.at[n, d], idx_rs.at[n, d], zpeer(d)) for n in (0, 1)] for d in far_z
    }
    idx_x = [
        remote(lists[2 + n], i_out.at[x, n], idx_ss.at[n, nz + d], idx_rs.at[n, nz + d], xpeer(d))
        for d in range(1, nx)
        for n in (0, 1)
    ]
    for pair in idx_z.values():
        for copy in pair:
            send(copy)
    twin = []
    for t in range(tiles):
        part = achip.at[t, pl.ds(core * width, width)]
        twin.append(
            remote(amp_ref.at[:, :, t * tile : (t + 1) * tile], part, sib_sem.at[0, t], sib_sem.at[1, t], sibling)
        )
        send(twin[t])
    first = {}
    for b in range(width):
        for d in far_first:
            to = lax.rem(y + d, ny)
            first[b, d] = remote(
                amp_ref.at[b, :, span(to, tile)],
                x_in.at[b, span(y, rows), :],
                y1_ss.at[b, d],
                y1_rs.at[b, d],
                ypeer(d),
            )
            send(first[b, d])
    for copy in idx_x:
        send(copy)
    shared = [remote(blk_ref.at[0], b_out.at[x], b_ss.at[d], b_rs.at[d], xpeer(d)) for d in range(1, nx)]
    for copy in shared:
        send(copy)

    for copy in own_tab[:2]:
        copy.wait()
    for t in range(tiles):
        own_amp[t].wait()
        twin[t].wait_recv()

    def slab(place, slot):
        win = idxs[place, 1, 0, slot]
        col = idxs[place, 0, 0, slot]
        return lax.div(win, per_chip), achip[col, lax.rem(win, per_chip)]

    moves = {}
    flying = [[], []]

    def z_message(direction, chain, hop):
        far = hops(direction, chain, nz)
        sign = 1 - 2 * direction
        dest = lax.rem(z + (sign * (far - hop) + nz) % nz, nz)
        for copy in idx_z.pop((sign * (hop - far) + nz) % nz, ()):
            copy.wait_recv()
        if hop == 0:
            buf = zinj.at[direction, chain]
        else:
            buf = zbuf.at[direction, chain, hop - 1]
            moves[direction, chain, hop - 1].wait_recv()
        if len(flying[direction]) == WINDOW:
            flying[direction].pop(0).wait_send()
        for k in range(CHUNK):
            owner, value = slab(dest, chain * CHUNK + k)
            if hop > 0:
                value = jnp.where(owner == z, value, buf[k])
            buf[k] = value
        moves[direction, chain, hop] = remote(
            buf,
            zbuf.at[direction, chain, hop],
            z_ss.at[direction, chain, hop],
            z_rs.at[direction, chain, hop],
            zpeer(sign),
        )
        flying[direction].append(moves[direction, chain, hop])
        flying[direction][-1].start()

    spread = {}

    def z_final(chain):
        last = [hops(direction, chain, nz) for direction in (0, 1)]
        for direction in (0, 1):
            moves[direction, chain, last[direction] - 1].wait_recv()
        for k in range(CHUNK):
            slot = chain * CHUNK + k
            owner, value = slab(z, slot)
            behind = lax.rem(z - owner + nz, nz)
            up = zbuf[0, chain, last[0] - 1, k]
            down = zbuf[1, chain, last[1] - 1, k]
            value = jnp.where(owner == z, value, jnp.where(behind <= last[0], up, down))
            sall[slot] = value
        part = sall.at[pl.ds(chain * CHUNK, CHUNK)]
        to = s_out.at[x, pl.ds(chain * CHUNK, CHUNK)]
        for d in (list(range(2, nx)) + [1]):
            spread[chain, d] = remote(part, to, s_ss.at[chain, d], s_rs.at[chain, d], xpeer(d))
            send(spread[chain, d])
        keep(pltpu.make_async_copy(part, to, own_sem.at[chain]))

    state = {"own": set(), "h": False}

    second = {}

    def hole(b, d):
        if b not in state["own"]:
            own_x[b].wait()
            for e in far_first:
                first[b, e].wait_recv()
            state["own"].add(b)
        if not state["h"]:
            own_h.wait()
            state["h"] = True
        to = lax.rem(y + d, ny)
        value = jnp.dot(hv[span(to, rows), :], x_in[b], preferred_element_type=jnp.float32)
        top = jnp.maximum(jnp.max(jnp.abs(value), axis=0, keepdims=True), LEAST)
        code = jnp.floor(value * (LEVELS / top) + 0.5)
        ysend[b, d] = code.astype(jnp.int32).astype(jnp.int16)
        ssend[b, d] = jnp.broadcast_to(top * (1.0 / LEVELS), ssend.shape[2:])
        pairs = ((ysend.at[b, d], y_out.at[b, y]), (ssend.at[b, d], r_out.at[b, y]))
        if d == 0:
            for n, (here, there) in enumerate(pairs):
                keep(pltpu.make_async_copy(here, there, own_sem.at[chains + 2 * b + n]))
            return
        second[b, d] = [
            remote(here, there, y2_ss.at[n, b, d], y2_rs.at[n, b, d], ypeer(d))
            for n, (here, there) in enumerate(pairs)
        ]
        for copy in second[b, d]:
            send(copy)

    runs = {"z": z_message, "f": z_final, "h": lambda b, n: hole(b, (far_first + [0])[n])}
    for kind, *place in plan(nz, chains, width, ny):
        runs[kind](*place)
    own_blk.wait()
    for copy in own_tab[2:] + kept:
        copy.wait()
    for copy in idx_x + shared + list(spread.values()) + [copy for pair in second.values() for copy in pair]:
        copy.wait_recv()
    for copy in sends + flying[0] + flying[1]:
        copy.wait_send()


def finish(idx_ref, win_ref, s_ref, b_ref, y_ref, r_ref, gap_ref, vir_ref, out_ref, s, b, y, r, gap, vir, acc, inv, out, idx, win, sem, more):
    origins, slots, rows, tile = s.shape
    width, tiles = y.shape[:2]
    x = lax.axis_index("rep")
    first = [
        pltpu.make_async_copy(here, there, sem.at[n])
        for n, (here, there) in enumerate(((gap_ref, gap), (vir_ref, vir), (y_ref, y), (r_ref, r)))
    ]
    first += [
        pltpu.make_async_copy(here, there, more.at[n]) for n, (here, there) in enumerate(((idx_ref, idx), (win_ref, win)))
    ]
    blocks = [
        [
            pltpu.make_async_copy(s_ref.at[o], s.at[o], sem.at[4 + 2 * o]),
            pltpu.make_async_copy(b_ref.at[o], b.at[o], sem.at[5 + 2 * o]),
        ]
        for o in range(origins)
    ]
    for copy in first + [copy for pair in blocks for copy in pair]:
        copy.start()
    for copy in first:
        copy.wait()
    column = jnp.transpose(jnp.broadcast_to(gap[...], (rows, tile)))
    for n in range(width):
        for t in range(tiles):
            acc[n * tiles + t] = y[n, t].astype(jnp.int32).astype(jnp.float32) * r[n, t, 0:1, :]
            inv[n * tiles + t] = 1.0 / (win[0, n] + column + vir[t : t + 1, :])
    for o in range(origins):
        for copy in blocks[o]:
            copy.wait()
        for k in range(slots):
            place = idx[o, 1, 0, k] * tiles + idx[o, 0, 0, k] - x * tiles
            inside = (idx[o, 0, 0, k] >= x * tiles) & (idx[o, 0, 0, k] < (x + 1) * tiles)
            place = jnp.where(inside, place, width * tiles)
            acc[place] += jnp.dot(s[o, k], b[o, k], preferred_element_type=jnp.float32)
    done = []
    for n in range(width):
        for t in range(tiles):
            out[n, :, t * tile : (t + 1) * tile] = acc[n * tiles + t] * inv[n * tiles + t]
        for half in range(2):
            part = pl.ds(half * rows // 2, rows // 2)
            done.append(
                pltpu.make_async_copy(out.at[n, part], out_ref.at[n, part], sem.at[4 + 2 * origins + 2 * n + half])
            )
            done[-1].start()
    for copy in done:
        copy.wait()


def local(
    amplitudes,
    pp_blocks,
    src_tiles,
    src_wins,
    dst_tiles,
    dst_wins,
    hh_integrals,
    pair_gap,
    vir_energy,
    win_energy,
):
    ny = lax.axis_size("amp")
    nz = lax.axis_size("int") // 2
    nx = lax.axis_size("rep")
    width, rows, ncol = amplitudes.shape
    tile = pp_blocks.shape[-1]
    slots = pp_blocks.shape[1]
    tiles = ncol // tile
    chains = slots // CHUNK
    bf, f32, i32 = jnp.bfloat16, jnp.float32, jnp.int32
    dma = pltpu.SemaphoreType.DMA
    hbm = pl.BlockSpec(memory_space=pltpu.HBM)
    slabs, blocks, codes, scales, places = pl.pallas_call(
        functools.partial(kernel, ny, nz, nx, chains),
        out_shape=[
            jax.ShapeDtypeStruct((nx, slots, rows, tile), bf),
            jax.ShapeDtypeStruct((nx, slots, tile, tile), bf),
            jax.ShapeDtypeStruct((width, ny, rows, tile), jnp.int16),
            jax.ShapeDtypeStruct((width, ny, 8, tile), f32),
            jax.ShapeDtypeStruct((nx, 2, 1, slots), i32),
        ],
        in_specs=[hbm] * 7,
        out_specs=[hbm] * 5,
        scratch_shapes=[
            pltpu.VMEM((tiles, 2 * width, rows, tile), bf),
            pltpu.VMEM((width, ny * rows, tile), bf),
            pltpu.VMEM(hh_integrals.shape, bf),
            pltpu.VMEM((slots, rows, tile), bf),
            pltpu.VMEM((2, chains, CHUNK, rows, tile), bf),
            pltpu.VMEM((2, chains, nz // 2, CHUNK, rows, tile), bf),
            pltpu.SMEM((nz, 2, 1, slots), i32),
            pltpu.VMEM((width, ny, rows, tile), jnp.int16),
            pltpu.VMEM((width, ny, 8, tile), f32),
            dma((4,)),
            dma((tiles,)),
            dma((8,)),
            dma((chains + 2 * width,)),
            dma((2, tiles)),
            dma((2, nz + nx)),
            dma((2, nz + nx)),
            dma((width, ny)),
            dma((width, ny)),
            dma((2, width, ny)),
            dma((2, width, ny)),
            dma((2, chains, nz // 2)),
            dma((2, chains, nz // 2)),
            dma((nx,)),
            dma((nx,)),
            dma((chains, nx)),
            dma((chains, nx)),
        ],
        compiler_params=pltpu.CompilerParams(
            collective_id=0, has_side_effects=True, vmem_limit_bytes=60 * 1024 * 1024
        ),
        cost_estimate=pl.CostEstimate(flops=700_000_000, bytes_accessed=5_000_000, transcendentals=0),
        name="ladder",
    )(src_tiles, src_wins, dst_tiles, dst_wins, amplitudes, pp_blocks, hh_integrals)
    return pl.pallas_call(
        finish,
        out_shape=jax.ShapeDtypeStruct((width, rows, ncol), f32),
        in_specs=[hbm] * 8,
        out_specs=hbm,
        scratch_shapes=[
            pltpu.VMEM(slabs.shape, bf),
            pltpu.VMEM(blocks.shape, bf),
            pltpu.VMEM(codes.shape, jnp.int16),
            pltpu.VMEM(scales.shape, f32),
            pltpu.VMEM((1, rows), f32),
            pltpu.VMEM((tiles, tile), f32),
            pltpu.VMEM((width * tiles + 1, rows, tile), f32),
            pltpu.VMEM((width * tiles, rows, tile), f32),
            pltpu.VMEM((width, rows, ncol), f32),
            pltpu.SMEM((nx, 2, 1, slots), i32),
            pltpu.SMEM((1, width), f32),
            dma((4 + 2 * nx + 2 * width,)),
            dma((2,)),
        ],
        compiler_params=pltpu.CompilerParams(vmem_limit_bytes=60 * 1024 * 1024),
        cost_estimate=pl.CostEstimate(flops=140_000_000, bytes_accessed=4_000_000, transcendentals=0),
        name="finish",
    )(
        places, win_energy.reshape(1, width), slabs, blocks, codes, scales,
        pair_gap.reshape(1, rows), vir_energy.reshape(tiles, tile),
    )


def solution(mesh):
    placed = (
        P("int", "amp", "rep"),
        P("rep", "int", None, None),
        P("rep", "int"),
        P("rep", "int"),
        P("rep", "int"),
        P("rep", "int"),
        P(),
        P("amp"),
        P("rep"),
        P("int"),
    )
    return jax.shard_map(
        local, mesh=mesh, in_specs=placed, out_specs=P("int", "amp", "rep"), check_vma=False
    )
```

```python
import functools

import jax
import jax.numpy as jnp
from jax import lax
from jax.experimental import pallas as pl
from jax.experimental.pallas import tpu as pltpu
from jax.sharding import PartitionSpec as P

MESH = pl.DeviceIdType.MESH
CHUNK = 1
LEVELS = 32760.0
LEAST = 1e-33
SLAB, DUE, APART, DELAY = 0.66, 6.0, 1.2, 2.5
START, COST_Z, COST_F, COST_H = 5.0, 0.12, 0.2, 0.45
POWER = 0.85
WINDOW = 4


def hops(direction, chain, nz):
    return nz // 2 - ((chain + direction) % 2)


def plan(nz, chains, width, ny):
    slab = SLAB * CHUNK
    todo = {}
    for j in range(chains):
        due = DUE + APART * j * CHUNK
        for d in (0, 1):
            far = hops(d, j, nz)
            for h in range(far):
                todo["z", d, j, h] = START + due * (2 * (h + 1 + nz // 2 - far) / nz) ** POWER
        todo["f", j] = START + due + DELAY
    landed = [2.0 + (b + 1) * ny * SLAB + DELAY for b in range(width)]
    for b in range(width):
        for n in range(ny):
            todo["h", b, n] = landed[b] + n * SLAB
    now, zfree, arrive, order = 0.0, [0.0, 0.0], {}, []

    def ready(k):
        if k[0] == "z":
            here = START if k[3] == 0 else arrive.get(("z", k[1], k[2], k[3] - 1), 1e9)
            return max(here, zfree[k[1]] - slab)
        if k[0] == "f":
            return max(arrive.get(("z", d, k[1], hops(d, k[1], nz) - 1), 1e9) for d in (0, 1))
        return landed[k[1]]

    while todo:
        when = {k: ready(k) for k in todo}
        open_now = [k for k in todo if when[k] <= now]
        if not open_now:
            now = min(when.values())
            continue
        k = min(open_now, key=lambda k: (todo[k], k))
        del todo[k]
        order.append(k)
        if k[0] == "z":
            now += COST_Z
            zfree[k[1]] = max(now, zfree[k[1]]) + slab
            arrive[k] = zfree[k[1]] + DELAY
        elif k[0] == "f":
            now += COST_F
        else:
            now += COST_H
    return order


def kernel(
    ny, nz, nx, chains,
    st_ref, sw_ref, dt_ref, dw_ref, amp_ref, blk_ref, h_ref,
    s_out, b_out, y_out, r_out, i_out,
    achip, x_in, hv, sall, zinj, zbuf, idxs, ysend, ssend, own,
    tab_sem, amp_sem, loc_sem, own_sem, sib_sem, idx_ss, idx_rs, y1_ss, y1_rs, y2_ss, y2_rs, z_ss, z_rs, b_ss, b_rs, s_ss, s_rs,
):
    width, rows, ncol = amp_ref.shape
    tile = blk_ref.shape[-1]
    tiles = ncol // tile
    per_chip = 2 * width
    slots = blk_ref.shape[1]
    y = lax.axis_index("amp")
    i = lax.axis_index("int")
    x = lax.axis_index("rep")
    z = i // 2
    core = lax.rem(i, 2)

    def ypeer(d):
        return {"amp": lax.rem(y + (d + ny) % ny, ny)}

    def zpeer(d):
        return {"int": lax.rem(i + 2 * ((d + nz) % nz), 2 * nz)}

    def xpeer(d):
        return {"rep": lax.rem(x + (d + nx) % nx, nx)}

    sibling = {"int": i + 1 - 2 * core}
    far_first = sorted(range(1, ny), key=lambda d: -min(d, ny - d))
    far_z = sorted(range(1, nz), key=lambda d: -min(d, nz - d))
    peers = [zpeer(d) for d in far_z] + [sibling] + [ypeer(d) for d in far_first]
    peers += [xpeer(d) for d in range(1, nx)]

    def remote(src, dst, ss, rs, peer):
        return pltpu.make_async_remote_copy(
            src_ref=src, dst_ref=dst, send_sem=ss, recv_sem=rs, device_id=peer, device_id_type=MESH
        )

    def span(index, size):
        return pl.ds(pl.multiple_of(index * size, size), size)

    sends = []

    kept = []

    def keep(copy):
        copy.start()
        kept.append(copy)

    def send(copy):
        copy.start()
        sends.append(copy)

    barrier = pltpu.get_barrier_semaphore()
    for peer in peers:
        pl.semaphore_signal(barrier, inc=1, device_id=peer, device_id_type=MESH)

    lists = (st_ref, sw_ref, dt_ref, dw_ref)
    own_tab = [
        pltpu.make_async_copy(ref, to, tab_sem.at[n])
        for n, (ref, to) in enumerate(zip(lists, (idxs.at[z, 0], idxs.at[z, 1], i_out.at[x, 0], i_out.at[x, 1])))
    ]
    own_amp = [
        pltpu.make_async_copy(
            amp_ref.at[:, :, t * tile : (t + 1) * tile], achip.at[t, pl.ds(core * width, width)], amp_sem.at[t]
        )
        for t in range(tiles)
    ]
    own_h = pltpu.make_async_copy(h_ref, hv, loc_sem.at[1])
    own_blk = pltpu.make_async_copy(blk_ref.at[0], own, loc_sem.at[2])
    own_x = [
        pltpu.make_async_copy(
            amp_ref.at[b, :, span(y, tile)], x_in.at[b, span(y, rows), :], loc_sem.at[3 + b]
        )
        for b in range(width)
    ]
    for copy in own_tab + own_x + own_amp + [own_h, own_blk]:
        copy.start()
    pl.semaphore_wait(barrier, len(peers))

    idx_z = {
        d: [remote(lists[n], idxs.at[z, n], idx_ss.at[n, d], idx_rs.at[n, d], zpeer(d)) for n in (0, 1)] for d in far_z
    }
    idx_x = [
        remote(lists[2 + n], i_out.at[x, n], idx_ss.at[n, nz + d], idx_rs.at[n, nz + d], xpeer(d))
        for d in range(1, nx)
        for n in (0, 1)
    ]
    for pair in idx_z.values():
        for copy in pair:
            send(copy)
    twin = []
    for t in range(tiles):
        part = achip.at[t, pl.ds(core * width, width)]
        twin.append(
            remote(amp_ref.at[:, :, t * tile : (t + 1) * tile], part, sib_sem.at[0, t], sib_sem.at[1, t], sibling)
        )
        send(twin[t])
    first = {}
    for b in range(width):
        for d in far_first:
            to = lax.rem(y + d, ny)
            first[b, d] = remote(
                amp_ref.at[b, :, span(to, tile)],
                x_in.at[b, span(y, rows), :],
                y1_ss.at[b, d],
                y1_rs.at[b, d],
                ypeer(d),
            )
            send(first[b, d])
    for copy in idx_x:
        send(copy)
    shared = [remote(blk_ref.at[0], b_out.at[x], b_ss.at[d], b_rs.at[d], xpeer(d)) for d in range(1, nx)]
    for copy in shared:
        send(copy)

    for copy in own_tab[:2] + [own_blk]:
        copy.wait()
    keep(pltpu.make_async_copy(own, b_out.at[x], loc_sem.at[7]))
    for t in range(tiles):
        own_amp[t].wait()
        twin[t].wait_recv()

    def slab(place, slot):
        win = idxs[place, 1, 0, slot]
        col = idxs[place, 0, 0, slot]
        return lax.div(win, per_chip), achip[col, lax.rem(win, per_chip)]

    moves = {}
    flying = [[], []]

    def z_message(direction, chain, hop):
        far = hops(direction, chain, nz)
        sign = 1 - 2 * direction
        dest = lax.rem(z + (sign * (far - hop) + nz) % nz, nz)
        for copy in idx_z.pop((sign * (hop - far) + nz) % nz, ()):
            copy.wait_recv()
        if hop == 0:
            buf = zinj.at[direction, chain]
        else:
            buf = zbuf.at[direction, chain, hop - 1]
            moves[direction, chain, hop - 1].wait_recv()
        if len(flying[direction]) == WINDOW:
            flying[direction].pop(0).wait_send()
        for k in range(CHUNK):
            owner, value = slab(dest, chain * CHUNK + k)
            if hop > 0:
                value = jnp.where(owner == z, value, buf[k])
            buf[k] = value
        moves[direction, chain, hop] = remote(
            buf,
            zbuf.at[direction, chain, hop],
            z_ss.at[direction, chain, hop],
            z_rs.at[direction, chain, hop],
            zpeer(sign),
        )
        flying[direction].append(moves[direction, chain, hop])
        flying[direction][-1].start()

    spread = {}

    def z_final(chain):
        last = [hops(direction, chain, nz) for direction in (0, 1)]
        for direction in (0, 1):
            moves[direction, chain, last[direction] - 1].wait_recv()
        for k in range(CHUNK):
            slot = chain * CHUNK + k
            owner, value = slab(z, slot)
            behind = lax.rem(z - owner + nz, nz)
            up = zbuf[0, chain, last[0] - 1, k]
            down = zbuf[1, chain, last[1] - 1, k]
            value = jnp.where(owner == z, value, jnp.where(behind <= last[0], up, down))
            sall[slot] = value
        part = sall.at[pl.ds(chain * CHUNK, CHUNK)]
        to = s_out.at[x, pl.ds(chain * CHUNK, CHUNK)]
        for d in (list(range(2, nx)) + [1]):
            spread[chain, d] = remote(part, to, s_ss.at[chain, d], s_rs.at[chain, d], xpeer(d))
            send(spread[chain, d])
        keep(pltpu.make_async_copy(part, to, own_sem.at[chain]))

    state = {"own": set(), "h": False}

    second = {}

    def hole(b, d):
        if b not in state["own"]:
            own_x[b].wait()
            for e in far_first:
                first[b, e].wait_recv()
            state["own"].add(b)
        if not state["h"]:
            own_h.wait()
            state["h"] = True
        to = lax.rem(y + d, ny)
        value = jnp.dot(hv[span(to, rows), :], x_in[b], preferred_element_type=jnp.float32)
        top = jnp.maximum(jnp.max(jnp.abs(value), axis=0, keepdims=True), LEAST)
        code = jnp.floor(value * (LEVELS / top) + 0.5)
        ysend[b, d] = code.astype(jnp.int32).astype(jnp.int16)
        ssend[b, d] = jnp.broadcast_to(top * (1.0 / LEVELS), ssend.shape[2:])
        pairs = ((ysend.at[b, d], y_out.at[b, y]), (ssend.at[b, d], r_out.at[b, y]))
        if d == 0:
            for n, (here, there) in enumerate(pairs):
                keep(pltpu.make_async_copy(here, there, own_sem.at[chains + 2 * b + n]))
            return
        second[b, d] = [
            remote(here, there, y2_ss.at[n, b, d], y2_rs.at[n, b, d], ypeer(d))
            for n, (here, there) in enumerate(pairs)
        ]
        for copy in second[b, d]:
            send(copy)

    runs = {"z": z_message, "f": z_final, "h": lambda b, n: hole(b, (far_first + [0])[n])}
    for kind, *place in plan(nz, chains, width, ny):
        runs[kind](*place)
    for copy in own_tab[2:] + kept:
        copy.wait()
    for copy in idx_x + shared + list(spread.values()) + [copy for pair in second.values() for copy in pair]:
        copy.wait_recv()
    for copy in sends + flying[0] + flying[1]:
        copy.wait_send()


def finish(idx_ref, win_ref, s_ref, b_ref, y_ref, r_ref, gap_ref, vir_ref, out_ref, s, b, y, r, gap, vir, acc, inv, out, idx, win, sem, more, out_sem):
    origins, slots, rows, tile = s.shape
    width, tiles = y.shape[:2]
    x = lax.axis_index("rep")
    first = [
        pltpu.make_async_copy(here, there, sem.at[n])
        for n, (here, there) in enumerate(((gap_ref, gap), (vir_ref, vir), (y_ref, y), (r_ref, r)))
    ]
    first += [
        pltpu.make_async_copy(here, there, more.at[n]) for n, (here, there) in enumerate(((idx_ref, idx), (win_ref, win)))
    ]
    blocks = [
        [
            pltpu.make_async_copy(s_ref.at[o], s.at[o], sem.at[4 + 2 * o]),
            pltpu.make_async_copy(b_ref.at[o], b.at[o], sem.at[5 + 2 * o]),
        ]
        for o in range(origins)
    ]
    for copy in first + [copy for pair in blocks for copy in pair]:
        copy.start()
    for copy in first:
        copy.wait()
    column = jnp.transpose(jnp.broadcast_to(gap[...], (rows, tile)))
    acc[width * tiles] = jnp.zeros((rows, tile), jnp.float32)
    for n in range(width):
        for t in range(tiles):
            acc[n * tiles + t] = y[n, t].astype(jnp.int32).astype(jnp.float32) * r[n, t, 0:1, :]
            inv[n * tiles + t] = 1.0 / (win[0, n] + column + vir[t : t + 1, :])
    for o in range(origins):
        for copy in blocks[o]:
            copy.wait()
        for k in range(slots):
            place = idx[o, 1, 0, k] * tiles + idx[o, 0, 0, k] - x * tiles
            inside = (idx[o, 0, 0, k] >= x * tiles) & (idx[o, 0, 0, k] < (x + 1) * tiles)
            place = jnp.where(inside, place, width * tiles)
            acc[place] += jnp.dot(s[o, k], b[o, k], preferred_element_type=jnp.float32)
    done = []
    for n in range(width):
        for t in range(tiles):
            o = n * tiles + t
            out[o] = acc[o] * inv[o]
            done.append(pltpu.make_async_copy(out.at[o], out_ref.at[n, :, t * tile : (t + 1) * tile], out_sem.at[o]))
            done[-1].start()
    for copy in done:
        copy.wait()


def local(
    amplitudes,
    pp_blocks,
    src_tiles,
    src_wins,
    dst_tiles,
    dst_wins,
    hh_integrals,
    pair_gap,
    vir_energy,
    win_energy,
):
    ny = lax.axis_size("amp")
    nz = lax.axis_size("int") // 2
    nx = lax.axis_size("rep")
    width, rows, ncol = amplitudes.shape
    tile = pp_blocks.shape[-1]
    slots = pp_blocks.shape[1]
    tiles = ncol // tile
    chains = slots // CHUNK
    bf, f32, i32 = jnp.bfloat16, jnp.float32, jnp.int32
    dma = pltpu.SemaphoreType.DMA
    hbm = pl.BlockSpec(memory_space=pltpu.HBM)
    slabs, blocks, codes, scales, places = pl.pallas_call(
        functools.partial(kernel, ny, nz, nx, chains),
        out_shape=[
            jax.ShapeDtypeStruct((nx, slots, rows, tile), bf),
            jax.ShapeDtypeStruct((nx, slots, tile, tile), bf),
            jax.ShapeDtypeStruct((width, ny, rows, tile), jnp.int16),
            jax.ShapeDtypeStruct((width, ny, 8, tile), f32),
            jax.ShapeDtypeStruct((nx, 2, 1, slots), i32),
        ],
        in_specs=[hbm] * 7,
        out_specs=[hbm] * 5,
        scratch_shapes=[
            pltpu.VMEM((tiles, 2 * width, rows, tile), bf),
            pltpu.VMEM((width, ny * rows, tile), bf),
            pltpu.VMEM(hh_integrals.shape, bf),
            pltpu.VMEM((slots, rows, tile), bf),
            pltpu.VMEM((2, chains, CHUNK, rows, tile), bf),
            pltpu.VMEM((2, chains, nz // 2, CHUNK, rows, tile), bf),
            pltpu.SMEM((nz, 2, 1, slots), i32),
            pltpu.VMEM((width, ny, rows, tile), jnp.int16),
            pltpu.VMEM((width, ny, 8, tile), f32),
            pltpu.VMEM((slots, tile, tile), bf),
            dma((4,)),
            dma((tiles,)),
            dma((8,)),
            dma((chains + 2 * width,)),
            dma((2, tiles)),
            dma((2, nz + nx)),
            dma((2, nz + nx)),
            dma((width, ny)),
            dma((width, ny)),
            dma((2, width, ny)),
            dma((2, width, ny)),
            dma((2, chains, nz // 2)),
            dma((2, chains, nz // 2)),
            dma((nx,)),
            dma((nx,)),
            dma((chains, nx)),
            dma((chains, nx)),
        ],
        compiler_params=pltpu.CompilerParams(
            collective_id=0, has_side_effects=True, vmem_limit_bytes=60 * 1024 * 1024
        ),
        cost_estimate=pl.CostEstimate(flops=700_000_000, bytes_accessed=5_000_000, transcendentals=0),
        name="ladder",
    )(src_tiles, src_wins, dst_tiles, dst_wins, amplitudes, pp_blocks, hh_integrals)
    return pl.pallas_call(
        finish,
        out_shape=jax.ShapeDtypeStruct((width, rows, ncol), f32),
        in_specs=[hbm] * 8,
        out_specs=hbm,
        scratch_shapes=[
            pltpu.VMEM(slabs.shape, bf),
            pltpu.VMEM(blocks.shape, bf),
            pltpu.VMEM(codes.shape, jnp.int16),
            pltpu.VMEM(scales.shape, f32),
            pltpu.VMEM((1, rows), f32),
            pltpu.VMEM((tiles, tile), f32),
            pltpu.VMEM((width * tiles + 1, rows, tile), f32),
            pltpu.VMEM((width * tiles, rows, tile), f32),
            pltpu.VMEM((width * tiles, rows, tile), f32),
            pltpu.SMEM((nx, 2, 1, slots), i32),
            pltpu.SMEM((1, width), f32),
            dma((4 + 2 * nx,)),
            dma((2,)),
            dma((width * tiles,)),
        ],
        compiler_params=pltpu.CompilerParams(vmem_limit_bytes=60 * 1024 * 1024),
        cost_estimate=pl.CostEstimate(flops=140_000_000, bytes_accessed=4_000_000, transcendentals=0),
        name="finish",
    )(
        places, win_energy.reshape(1, width), slabs, blocks, codes, scales,
        pair_gap.reshape(1, rows), vir_energy.reshape(tiles, tile),
    )


def solution(mesh):
    placed = (
        P("int", "amp", "rep"),
        P("rep", "int", None, None),
        P("rep", "int"),
        P("rep", "int"),
        P("rep", "int"),
        P("rep", "int"),
        P(),
        P("amp"),
        P("rep"),
        P("int"),
    )
    return jax.shard_map(
        local, mesh=mesh, in_specs=placed, out_specs=P("int", "amp", "rep"), check_vma=False
    )
```

```python
import functools

import jax
import jax.numpy as jnp
from jax import lax
from jax.experimental import pallas as pl
from jax.experimental.pallas import tpu as pltpu
from jax.sharding import PartitionSpec as P

MESH = pl.DeviceIdType.MESH
CHUNK = 1
LEVELS = 32760.0
LEAST = 1e-33
SLAB, DUE, APART, DELAY = 0.66, 6.0, 1.2, 2.5
START, COST_Z, COST_F, COST_H = 5.0, 0.12, 0.2, 0.45
POWER = 0.85
WINDOW = 5


def hops(direction, chain, nz):
    return nz // 2 - ((chain + direction) % 2)


def plan(nz, chains, width, ny):
    slab = SLAB * CHUNK
    todo = {}
    for j in range(chains):
        due = DUE + APART * j * CHUNK
        for d in (0, 1):
            far = hops(d, j, nz)
            for h in range(far):
                todo["z", d, j, h] = START + due * (2 * (h + 1 + nz // 2 - far) / nz) ** POWER
        todo["f", j] = START + due + DELAY
    landed = [2.0 + (b + 1) * ny * SLAB + DELAY for b in range(width)]
    for b in range(width):
        for n in range(ny):
            todo["h", b, n] = landed[b] + n * SLAB
    now, zfree, arrive, order = 0.0, [0.0, 0.0], {}, []

    def ready(k):
        if k[0] == "z":
            here = START if k[3] == 0 else arrive.get(("z", k[1], k[2], k[3] - 1), 1e9)
            return max(here, zfree[k[1]] - slab)
        if k[0] == "f":
            return max(arrive.get(("z", d, k[1], hops(d, k[1], nz) - 1), 1e9) for d in (0, 1))
        return landed[k[1]]

    while todo:
        when = {k: ready(k) for k in todo}
        open_now = [k for k in todo if when[k] <= now]
        if not open_now:
            now = min(when.values())
            continue
        k = min(open_now, key=lambda k: (todo[k], k))
        del todo[k]
        order.append(k)
        if k[0] == "z":
            now += COST_Z
            zfree[k[1]] = max(now, zfree[k[1]]) + slab
            arrive[k] = zfree[k[1]] + DELAY
        elif k[0] == "f":
            now += COST_F
        else:
            now += COST_H
    return order


def kernel(
    ny, nz, nx, chains,
    st_ref, sw_ref, dt_ref, dw_ref, amp_ref, blk_ref, h_ref,
    s_out, b_out, y_out, r_out, i_out,
    achip, x_in, hv, sall, zinj, zbuf, idxs, ysend, ssend, own,
    tab_sem, amp_sem, loc_sem, own_sem, sib_sem, idx_ss, idx_rs, y1_ss, y1_rs, y2_ss, y2_rs, z_ss, z_rs, b_ss, b_rs, s_ss, s_rs,
):
    width, rows, ncol = amp_ref.shape
    tile = blk_ref.shape[-1]
    tiles = ncol // tile
    per_chip = 2 * width
    slots = blk_ref.shape[1]
    y = lax.axis_index("amp")
    i = lax.axis_index("int")
    x = lax.axis_index("rep")
    z = i // 2
    core = lax.rem(i, 2)

    def ypeer(d):
        return {"amp": lax.rem(y + (d + ny) % ny, ny)}

    def zpeer(d):
        return {"int": lax.rem(i + 2 * ((d + nz) % nz), 2 * nz)}

    def xpeer(d):
        return {"rep": lax.rem(x + (d + nx) % nx, nx)}

    sibling = {"int": i + 1 - 2 * core}
    far_first = sorted(range(1, ny), key=lambda d: -min(d, ny - d))
    far_z = sorted(range(1, nz), key=lambda d: -min(d, nz - d))
    peers = [zpeer(d) for d in far_z] + [sibling] + [ypeer(d) for d in far_first]
    peers += [xpeer(d) for d in range(1, nx)]

    def remote(src, dst, ss, rs, peer):
        return pltpu.make_async_remote_copy(
            src_ref=src, dst_ref=dst, send_sem=ss, recv_sem=rs, device_id=peer, device_id_type=MESH
        )

    def span(index, size):
        return pl.ds(pl.multiple_of(index * size, size), size)

    sends = []

    kept = []

    def keep(copy):
        copy.start()
        kept.append(copy)

    def send(copy):
        copy.start()
        sends.append(copy)

    barrier = pltpu.get_barrier_semaphore()
    for peer in peers:
        pl.semaphore_signal(barrier, inc=1, device_id=peer, device_id_type=MESH)

    lists = (st_ref, sw_ref, dt_ref, dw_ref)
    own_tab = [
        pltpu.make_async_copy(ref, to, tab_sem.at[n])
        for n, (ref, to) in enumerate(zip(lists, (idxs.at[z, 0], idxs.at[z, 1], i_out.at[x, 0], i_out.at[x, 1])))
    ]
    own_amp = [
        pltpu.make_async_copy(
            amp_ref.at[:, :, t * tile : (t + 1) * tile], achip.at[t, pl.ds(core * width, width)], amp_sem.at[t]
        )
        for t in range(tiles)
    ]
    own_h = pltpu.make_async_copy(h_ref, hv, loc_sem.at[1])
    own_blk = pltpu.make_async_copy(blk_ref.at[0], own, loc_sem.at[2])
    own_x = [
        pltpu.make_async_copy(
            amp_ref.at[b, :, span(y, tile)], x_in.at[b, span(y, rows), :], loc_sem.at[3 + b]
        )
        for b in range(width)
    ]
    for copy in own_tab + own_x + own_amp + [own_h, own_blk]:
        copy.start()
    pl.semaphore_wait(barrier, len(peers))

    idx_z = {
        d: [remote(lists[n], idxs.at[z, n], idx_ss.at[n, d], idx_rs.at[n, d], zpeer(d)) for n in (0, 1)] for d in far_z
    }
    idx_x = [
        remote(lists[2 + n], i_out.at[x, n], idx_ss.at[n, nz + d], idx_rs.at[n, nz + d], xpeer(d))
        for d in range(1, nx)
        for n in (0, 1)
    ]
    for pair in idx_z.values():
        for copy in pair:
            send(copy)
    twin = []
    for t in range(tiles):
        part = achip.at[t, pl.ds(core * width, width)]
        twin.append(
            remote(amp_ref.at[:, :, t * tile : (t + 1) * tile], part, sib_sem.at[0, t], sib_sem.at[1, t], sibling)
        )
        send(twin[t])
    first = {}
    for b in range(width):
        for d in far_first:
            to = lax.rem(y + d, ny)
            first[b, d] = remote(
                amp_ref.at[b, :, span(to, tile)],
                x_in.at[b, span(y, rows), :],
                y1_ss.at[b, d],
                y1_rs.at[b, d],
                ypeer(d),
            )
            send(first[b, d])
    for copy in idx_x:
        send(copy)
    shared = [remote(blk_ref.at[0], b_out.at[x], b_ss.at[d], b_rs.at[d], xpeer(d)) for d in range(1, nx)]
    for copy in shared:
        send(copy)

    for copy in own_tab[:2] + [own_blk]:
        copy.wait()
    keep(pltpu.make_async_copy(own, b_out.at[x], loc_sem.at[7]))
    for t in range(tiles):
        own_amp[t].wait()
        twin[t].wait_recv()

    def slab(place, slot):
        win = idxs[place, 1, 0, slot]
        col = idxs[place, 0, 0, slot]
        return lax.div(win, per_chip), achip[col, lax.rem(win, per_chip)]

    moves = {}
    flying = [[], []]

    def z_message(direction, chain, hop):
        far = hops(direction, chain, nz)
        sign = 1 - 2 * direction
        dest = lax.rem(z + (sign * (far - hop) + nz) % nz, nz)
        for copy in idx_z.pop((sign * (hop - far) + nz) % nz, ()):
            copy.wait_recv()
        if hop == 0:
            buf = zinj.at[direction, chain]
        else:
            buf = zbuf.at[direction, chain, hop - 1]
            moves[direction, chain, hop - 1].wait_recv()
        if len(flying[direction]) == WINDOW:
            flying[direction].pop(0).wait_send()
        for k in range(CHUNK):
            owner, value = slab(dest, chain * CHUNK + k)
            if hop > 0:
                value = jnp.where(owner == z, value, buf[k])
            buf[k] = value
        moves[direction, chain, hop] = remote(
            buf,
            zbuf.at[direction, chain, hop],
            z_ss.at[direction, chain, hop],
            z_rs.at[direction, chain, hop],
            zpeer(sign),
        )
        flying[direction].append(moves[direction, chain, hop])
        flying[direction][-1].start()

    spread = {}

    def z_final(chain):
        last = [hops(direction, chain, nz) for direction in (0, 1)]
        for direction in (0, 1):
            moves[direction, chain, last[direction] - 1].wait_recv()
        for k in range(CHUNK):
            slot = chain * CHUNK + k
            owner, value = slab(z, slot)
            behind = lax.rem(z - owner + nz, nz)
            up = zbuf[0, chain, last[0] - 1, k]
            down = zbuf[1, chain, last[1] - 1, k]
            value = jnp.where(owner == z, value, jnp.where(behind <= last[0], up, down))
            sall[slot] = value
        part = sall.at[pl.ds(chain * CHUNK, CHUNK)]
        to = s_out.at[x, pl.ds(chain * CHUNK, CHUNK)]
        for d in (list(range(2, nx)) + [1]):
            spread[chain, d] = remote(part, to, s_ss.at[chain, d], s_rs.at[chain, d], xpeer(d))
            send(spread[chain, d])
        keep(pltpu.make_async_copy(part, to, own_sem.at[chain]))

    state = {"own": set(), "h": False}

    second = {}

    def hole(b, d):
        if b not in state["own"]:
            own_x[b].wait()
            for e in far_first:
                first[b, e].wait_recv()
            state["own"].add(b)
        if not state["h"]:
            own_h.wait()
            state["h"] = True
        to = lax.rem(y + d, ny)
        value = jnp.dot(hv[span(to, rows), :], x_in[b], preferred_element_type=jnp.float32)
        top = jnp.maximum(jnp.max(jnp.abs(value), axis=0, keepdims=True), LEAST)
        code = jnp.floor(value * (LEVELS / top) + 0.5)
        ysend[b, d] = code.astype(jnp.int32).astype(jnp.int16)
        ssend[b, d] = jnp.broadcast_to(top * (1.0 / LEVELS), ssend.shape[2:])
        pairs = ((ysend.at[b, d], y_out.at[b, y]), (ssend.at[b, d], r_out.at[b, y]))
        if d == 0:
            for n, (here, there) in enumerate(pairs):
                keep(pltpu.make_async_copy(here, there, own_sem.at[chains + 2 * b + n]))
            return
        second[b, d] = [
            remote(here, there, y2_ss.at[n, b, d], y2_rs.at[n, b, d], ypeer(d))
            for n, (here, there) in enumerate(pairs)
        ]
        for copy in second[b, d]:
            send(copy)

    runs = {"z": z_message, "f": z_final, "h": lambda b, n: hole(b, (far_first + [0])[n])}
    for kind, *place in plan(nz, chains, width, ny):
        runs[kind](*place)
    for copy in own_tab[2:] + kept:
        copy.wait()
    for copy in idx_x + shared + list(spread.values()) + [copy for pair in second.values() for copy in pair]:
        copy.wait_recv()
    for copy in sends + flying[0] + flying[1]:
        copy.wait_send()


def finish(idx_ref, win_ref, s_ref, b_ref, y_ref, r_ref, gap_ref, vir_ref, out_ref, s, b, y, r, gap, vir, acc, inv, out, idx, win, sem, more, out_sem):
    origins, slots, rows, tile = s.shape
    width, tiles = y.shape[:2]
    x = lax.axis_index("rep")
    first = [
        pltpu.make_async_copy(here, there, sem.at[n])
        for n, (here, there) in enumerate(((gap_ref, gap), (vir_ref, vir), (y_ref, y), (r_ref, r)))
    ]
    first += [
        pltpu.make_async_copy(here, there, more.at[n]) for n, (here, there) in enumerate(((idx_ref, idx), (win_ref, win)))
    ]
    blocks = [
        [
            pltpu.make_async_copy(s_ref.at[o], s.at[o], sem.at[4 + 2 * o]),
            pltpu.make_async_copy(b_ref.at[o], b.at[o], sem.at[5 + 2 * o]),
        ]
        for o in range(origins)
    ]
    for copy in first + [copy for pair in blocks for copy in pair]:
        copy.start()
    for copy in first:
        copy.wait()
    column = jnp.transpose(jnp.broadcast_to(gap[...], (rows, tile)))
    acc[width * tiles] = jnp.zeros((rows, tile), jnp.float32)
    for n in range(width):
        for t in range(tiles):
            acc[n * tiles + t] = y[n, t].astype(jnp.int32).astype(jnp.float32) * r[n, t, 0:1, :]
            inv[n * tiles + t] = 1.0 / (win[0, n] + column + vir[t : t + 1, :])
    for o in range(origins):
        for copy in blocks[o]:
            copy.wait()
        for k in range(slots):
            place = idx[o, 1, 0, k] * tiles + idx[o, 0, 0, k] - x * tiles
            inside = (idx[o, 0, 0, k] >= x * tiles) & (idx[o, 0, 0, k] < (x + 1) * tiles)
            place = jnp.where(inside, place, width * tiles)
            acc[place] += jnp.dot(s[o, k], b[o, k], preferred_element_type=jnp.float32)
    done = []
    for n in range(width):
        for t in range(tiles):
            o = n * tiles + t
            out[o] = acc[o] * inv[o]
            done.append(pltpu.make_async_copy(out.at[o], out_ref.at[n, :, t * tile : (t + 1) * tile], out_sem.at[o]))
            done[-1].start()
    for copy in done:
        copy.wait()


def local(
    amplitudes,
    pp_blocks,
    src_tiles,
    src_wins,
    dst_tiles,
    dst_wins,
    hh_integrals,
    pair_gap,
    vir_energy,
    win_energy,
):
    ny = lax.axis_size("amp")
    nz = lax.axis_size("int") // 2
    nx = lax.axis_size("rep")
    width, rows, ncol = amplitudes.shape
    tile = pp_blocks.shape[-1]
    slots = pp_blocks.shape[1]
    tiles = ncol // tile
    chains = slots // CHUNK
    bf, f32, i32 = jnp.bfloat16, jnp.float32, jnp.int32
    dma = pltpu.SemaphoreType.DMA
    hbm = pl.BlockSpec(memory_space=pltpu.HBM)
    slabs, blocks, codes, scales, places = pl.pallas_call(
        functools.partial(kernel, ny, nz, nx, chains),
        out_shape=[
            jax.ShapeDtypeStruct((nx, slots, rows, tile), bf),
            jax.ShapeDtypeStruct((nx, slots, tile, tile), bf),
            jax.ShapeDtypeStruct((width, ny, rows, tile), jnp.int16),
            jax.ShapeDtypeStruct((width, ny, 8, tile), f32),
            jax.ShapeDtypeStruct((nx, 2, 1, slots), i32),
        ],
        in_specs=[hbm] * 7,
        out_specs=[hbm] * 5,
        scratch_shapes=[
            pltpu.VMEM((tiles, 2 * width, rows, tile), bf),
            pltpu.VMEM((width, ny * rows, tile), bf),
            pltpu.VMEM(hh_integrals.shape, bf),
            pltpu.VMEM((slots, rows, tile), bf),
            pltpu.VMEM((2, chains, CHUNK, rows, tile), bf),
            pltpu.VMEM((2, chains, nz // 2, CHUNK, rows, tile), bf),
            pltpu.SMEM((nz, 2, 1, slots), i32),
            pltpu.VMEM((width, ny, rows, tile), jnp.int16),
            pltpu.VMEM((width, ny, 8, tile), f32),
            pltpu.VMEM((slots, tile, tile), bf),
            dma((4,)),
            dma((tiles,)),
            dma((8,)),
            dma((chains + 2 * width,)),
            dma((2, tiles)),
            dma((2, nz + nx)),
            dma((2, nz + nx)),
            dma((width, ny)),
            dma((width, ny)),
            dma((2, width, ny)),
            dma((2, width, ny)),
            dma((2, chains, nz // 2)),
            dma((2, chains, nz // 2)),
            dma((nx,)),
            dma((nx,)),
            dma((chains, nx)),
            dma((chains, nx)),
        ],
        compiler_params=pltpu.CompilerParams(
            collective_id=0, has_side_effects=True, vmem_limit_bytes=60 * 1024 * 1024
        ),
        cost_estimate=pl.CostEstimate(flops=700_000_000, bytes_accessed=5_000_000, transcendentals=0),
        name="ladder",
    )(src_tiles, src_wins, dst_tiles, dst_wins, amplitudes, pp_blocks, hh_integrals)
    return pl.pallas_call(
        finish,
        out_shape=jax.ShapeDtypeStruct((width, rows, ncol), f32),
        in_specs=[hbm] * 8,
        out_specs=hbm,
        scratch_shapes=[
            pltpu.VMEM(slabs.shape, bf),
            pltpu.VMEM(blocks.shape, bf),
            pltpu.VMEM(codes.shape, jnp.int16),
            pltpu.VMEM(scales.shape, f32),
            pltpu.VMEM((1, rows), f32),
            pltpu.VMEM((tiles, tile), f32),
            pltpu.VMEM((width * tiles + 1, rows, tile), f32),
            pltpu.VMEM((width * tiles, rows, tile), f32),
            pltpu.VMEM((width * tiles, rows, tile), f32),
            pltpu.SMEM((nx, 2, 1, slots), i32),
            pltpu.SMEM((1, width), f32),
            dma((4 + 2 * nx,)),
            dma((2,)),
            dma((width * tiles,)),
        ],
        compiler_params=pltpu.CompilerParams(vmem_limit_bytes=60 * 1024 * 1024),
        cost_estimate=pl.CostEstimate(flops=140_000_000, bytes_accessed=4_000_000, transcendentals=0),
        name="finish",
    )(
        places, win_energy.reshape(1, width), slabs, blocks, codes, scales,
        pair_gap.reshape(1, rows), vir_energy.reshape(tiles, tile),
    )


def solution(mesh):
    placed = (
        P("int", "amp", "rep"),
        P("rep", "int", None, None),
        P("rep", "int"),
        P("rep", "int"),
        P("rep", "int"),
        P("rep", "int"),
        P(),
        P("amp"),
        P("rep"),
        P("int"),
    )
    return jax.shard_map(
        local, mesh=mesh, in_specs=placed, out_specs=P("int", "amp", "rep"), check_vma=False
    )
```
